256 devices in a mesh: dp: 64 (over x_lo, y, z), tensor: 4 (over x_hi, core).
Axes of the slice: x: 4 (x_hi: 2, x_lo: 2; x = x_hi * 2 + x_lo), y: 4, z: 8, core: 2. Of those that a mesh axis runs over, the one named last changes fastest.
Arguments:
- attn: bfloat16 [16384, 8192], P('dp', 'tensor'), may hold values from -6 to 6
- output_gradient: bfloat16 [16384, 8192], P(('dp', 'tensor')), may hold values from -0.29882812 to 0.29882812
- down_weight: bfloat16 [512, 8192], P('dp', 'tensor'), may hold values from -0.0625 to 0.0625
- up_weight: bfloat16 [512, 8192], P('dp', 'tensor'), may hold values from -0.0625 to 0.0625
- adapter_of_row: int32 [16384], P('dp'), may hold values from -1 to 31, as said below
- lengths: int32 [64], P('dp'), may hold values from 1 to 256, 12288 in all
Outputs:
- attention_gradient: bfloat16 [16384, 8192], P('dp', 'tensor')
- grad_a: float32 [512, 8192], P('dp', 'tensor')
- grad_b: float32 [512, 8192], P('dp', 'tensor')
The draws below stay inside these ranges and needn't reach their ends.
Inputs may be any that keep to these rules, and one draw needn't show every extreme that they name: `adapter_of_row`: within each aligned block of 128 rows the first 32 to 128 rows carry one adapter id and the rest are -1; along the rows of one sequence the blocks' ids never fall.
All inputs are finite; a program needn't handle non-finite values. No bound on the sum of `lengths` on one device may be relied on, other than what follows from the above.
Results may differ from the reference program's by a relative error of at most 0.0049.
Values may be sent and summed in bfloat16 or wider, within the bound.
No kernel may reach another device: no remote copies, remote signals or barrier semaphores. Data moves between devices by JAX's collectives and lax.ppermute only.
A program may use at most 64 MiB of HBM per device.

```python
import math
import jax
import jax.numpy as jnp
import numpy as np
from jax import lax

MODEL_WIDTH = 8192
ADAPTER_COUNT = 32
ADAPTER_RANK = 16
TOK_DEV = 256
SEQS = 64
TOKENS = 16384
N_DP = 64


def draw_adapter_of_row(key, part):
    key = jax.random.fold_in(key, 7)
    first, second = jax.random.split(key)
    sequences = TOKENS // TOK_DEV
    blocks = TOK_DEV // 128
    labels = jax.random.randint(first, (sequences, blocks), 0, ADAPTER_COUNT)
    labels = jnp.sort(labels, axis=1)
    labels = labels.at[0, blocks - 1].set(ADAPTER_COUNT - 1)
    filled = jax.random.randint(second, (sequences, blocks), 32, 129)
    offsets = jnp.arange(128)
    row_count = jnp.where(offsets[None, None, :] < filled[:, :, None], labels[:, :, None], -1)
    return row_count.reshape(TOKENS).astype(jnp.int32)


def shard_levels(rng, extent, pieces, smallest, top_value):
    factor_of = 1.0
    for dim, blocks in pieces:
        steps = jax.random.uniform(jax.random.fold_in(jax.random.fold_in(rng, 6), dim), (blocks,), jnp.float32, smallest / len(pieces), top_value / len(pieces))
        factor_of = factor_of * jnp.repeat(jnp.exp(steps), extent[dim] // blocks).reshape((-1,) + (1,) * (len(extent) - 1 - dim))
    return factor_of


def split_up(amount, total, bound, slope):
    weights = [(1 << 20) // math.isqrt(grade ** slope) + 1 for grade in range(2, amount + 1)]
    rest, given = total - bound - (amount - 1), [1] * (amount - 1)
    while rest > 0:
        candidates = [i for i in range(amount - 1) if given[i] < bound]
        whole, remaining = sum([weights[i] for i in candidates]), rest
        for i in candidates:
            extra = min(bound - given[i], max(1, remaining * weights[i] // whole), rest)
            given[i] = given[i] + extra
            rest = rest - extra
    return np.array([bound] + given)


def ragged_sizes(own_key, amount, total, reach, skew):
    if amount == 2:
        one = jax.random.randint(own_key, (), max(1, total - reach), min(reach, total - 1) + 1)
        return jnp.stack([one, total - one])
    tallies = jnp.asarray(split_up(amount, total, reach, skew), jnp.int32)
    couples = (amount - 1) // 2
    source_of, receiver = tallies[1:1 + 2 * couples:2], tallies[2:2 + 2 * couples:2]
    slack = jnp.minimum(source_of - 1, reach - receiver)
    moved = jax.random.randint(jax.random.fold_in(own_key, 1), (couples,), 0, 1 << 20) % (slack + 1)
    tallies = tallies.at[1:1 + 2 * couples:2].set(source_of - moved).at[2:2 + 2 * couples:2].set(receiver + moved)
    return tallies[jax.random.permutation(jax.random.fold_in(own_key, 2), amount)]


def bell_draw(key, dims, spread, most, shards=(), kind=jnp.bfloat16):
    drawn = spread * jax.random.normal(key, dims, jnp.float32)
    if shards:
        drawn = drawn * shard_levels(key, dims, shards, -0.22, 0.18)
    return jnp.clip(drawn, -most, most).astype(kind)


def setup_inputs(seed: int = 0) -> dict:
    splits = jax.random.split(jax.random.key(seed), 7)
    return {
        "attn": bell_draw(splits[0], (TOKENS, MODEL_WIDTH), 1.0, 6.0, ((0, 64), (1, 4))),
        "output_gradient": bell_draw(splits[1], (TOKENS, MODEL_WIDTH), 0.05, 0.29882812, ((0, 256),)),
        "down_weight": bell_draw(splits[2], (ADAPTER_COUNT * ADAPTER_RANK, MODEL_WIDTH), MODEL_WIDTH ** -0.5, 0.0625, ((0, 64), (1, 4))),
        "up_weight": bell_draw(splits[3], (ADAPTER_COUNT * ADAPTER_RANK, MODEL_WIDTH), MODEL_WIDTH ** -0.5, 0.0625, ((0, 64), (1, 4))),
        "adapter_of_row": draw_adapter_of_row(jax.random.fold_in(splits[6], 71), 0),
        "lengths": ragged_sizes(splits[5], SEQS, N_DP * TOK_DEV * 3 // 4, TOK_DEV, 1).astype(jnp.int32),
    }


adapter_scale = 2.0


def reference(attn, output_gradient, down_weight, up_weight, adapter_of_row, lengths):
    per_seq = TOK_DEV // 128
    count = TOKENS // 128
    down_table = down_weight.reshape(ADAPTER_COUNT, ADAPTER_RANK, MODEL_WIDTH)
    up_table = up_weight.reshape(ADAPTER_COUNT, ADAPTER_RANK, MODEL_WIDTH)

    def step(carry, block):
        acc_a, acc_b = carry
        start = (block * 128).astype(jnp.int32)
        input_rows = lax.dynamic_slice_in_dim(attn, start, 128, 0)
        gradient_list = lax.dynamic_slice_in_dim(output_gradient, start, 128, 0)
        labels = lax.dynamic_slice_in_dim(adapter_of_row, start, 128, 0)
        sequence = (block // per_seq).astype(jnp.int32)
        offsets = (block % per_seq).astype(jnp.int32) * 128 + jnp.arange(128, dtype=jnp.int32)
        live = (labels >= 0) & (offsets < lengths[sequence])
        gradient_list = jnp.where(live[:, None], gradient_list, jnp.zeros_like(gradient_list))
        which = jnp.maximum(labels[0], 0)
        down_projected = down_table[which]
        upper = up_table[which]
        inner_product = jnp.dot(input_rows, down_projected.T, preferred_element_type=jnp.float32).astype(jnp.bfloat16)
        outer_product = jnp.dot(gradient_list, upper.T, preferred_element_type=jnp.float32).astype(jnp.bfloat16)
        backward_pass = (adapter_scale * jnp.dot(outer_product, down_projected, preferred_element_type=jnp.float32)).astype(jnp.bfloat16)
        down_term = adapter_scale * jnp.dot(outer_product.T, input_rows, preferred_element_type=jnp.float32)
        up_term = adapter_scale * jnp.dot(inner_product.T, gradient_list, preferred_element_type=jnp.float32)
        acc_a = acc_a.at[which].add(down_term)
        acc_b = acc_b.at[which].add(up_term)
        return (acc_a, acc_b), backward_pass

    start_acc = (jnp.zeros((ADAPTER_COUNT, ADAPTER_RANK, MODEL_WIDTH), jnp.float32), jnp.zeros((ADAPTER_COUNT, ADAPTER_RANK, MODEL_WIDTH), jnp.float32))
    (acc_a, acc_b), backs = lax.scan(step, start_acc, jnp.arange(count, dtype=jnp.int32))
    attention_gradient = backs.reshape(TOKENS, MODEL_WIDTH)
    return attention_gradient, acc_a.reshape(ADAPTER_COUNT * ADAPTER_RANK, MODEL_WIDTH), acc_b.reshape(ADAPTER_COUNT * ADAPTER_RANK, MODEL_WIDTH)
```

```python
import jax
import jax.numpy as jnp
from jax import lax
from jax.experimental import pallas as pl
from jax.experimental.pallas import tpu as pltpu
from jax.sharding import PartitionSpec as P

LANES = 128
BLOCK = 128
PEERS = 64
BANDS = 16
QUARTERS = 4

F32 = jnp.float32
BF16 = jnp.bfloat16

adapter_scale = 2.0

VMEM = pl.BlockSpec(memory_space=pltpu.VMEM)
SMEM = pl.BlockSpec(memory_space=pltpu.SMEM)
PARAMS = pltpu.CompilerParams(vmem_limit_bytes=40 * 1024 * 1024)


def rows_of(first, size, stride):
    return pl.ds(first, size, stride=stride)


def pack_tables(down_ref, up_ref, label_ref, out_ref, rows_f, out_f):
    for m, map_ref in enumerate((down_ref, up_ref)):
        for c in range(BANDS):
            rows_f[c * 8:(c + 1) * 8, :] = map_ref[:, c * LANES:(c + 1) * LANES].astype(F32)
        for i in range(2):
            out_f[rows_of(2 * m + i, PEERS, 8), :] = rows_f[rows_of(i, PEERS, 2), :]
    for b in range(2):
        which = jnp.maximum(label_ref[b * BLOCK], 0).astype(F32)
        out_f[rows_of(4 + b, PEERS, 8), :] = jnp.full((PEERS, LANES), which, F32)
        out_f[rows_of(6 + b, PEERS, 8), :] = jnp.zeros((PEERS, LANES), F32)
    out_ref[...] = out_f[...].astype(BF16)


def pick_rows(in_ref, out_ref, in_f, out_f):
    in_f[...] = in_ref[...].astype(F32)
    table = jnp.concatenate([in_f[rows_of(k, PEERS, 8), :] for k in range(4)], axis=1).astype(BF16)
    lane = lax.broadcasted_iota(jnp.int32, (PEERS, LANES), 1)
    for b in range(2):
        which = in_f[rows_of(4 + b, PEERS, 8), :].astype(jnp.int32)
        for h in range(2):
            chosen = (lane == 2 * which + h).astype(F32).astype(BF16)[:, :PEERS]
            picked = jnp.dot(chosen, table, preferred_element_type=F32)
            for k in range(4):
                out_f[rows_of(b * 8 + h * 4 + k, PEERS, 16), :] = picked[:, k * LANES:(k + 1) * LANES]
    out_ref[...] = out_f[...].astype(BF16)


def project(picked_ref, attn_ref, own_ref, one_ref, two_ref, three_ref, place_ref, maps_ref, grad_ref, part_ref):
    me = place_ref[0]
    for k, piece in enumerate((own_ref, one_ref, two_ref, three_ref)):
        first = pl.multiple_of(lax.bitwise_xor(me, k) * 64, 64)
        grad_ref[pl.ds(first, 64), :] = piece[...]
    for c in range(BANDS):
        rows = picked_ref[c * 64:(c + 1) * 64, :].astype(F32).reshape(QUARTERS, 2, 8, LANES)
        for b in range(2):
            maps_ref[b * 32:(b + 1) * 32, c * LANES:(c + 1) * LANES] = rows[:, b].reshape(32, LANES).astype(BF16)
    row = lax.broadcasted_iota(jnp.int32, (32, BLOCK), 0)
    over_last = (((1,), (1,)), ((), ()))
    for b in range(2):
        maps = maps_ref[b * 32:(b + 1) * 32, :]
        block = slice(b * BLOCK, (b + 1) * BLOCK)
        inner = lax.dot_general(maps, attn_ref[block, :], over_last, preferred_element_type=F32)
        outer = lax.dot_general(maps, grad_ref[block, :], over_last, preferred_element_type=F32)
        part_ref[:, block] = jnp.where((row & 2) == 0, inner, outer)


def expand(own_ref, one_ref, two_ref, three_ref, label_ref, length_ref, maps_ref, attn_ref, grad_ref, back_ref, term_ref):
    total = (own_ref[...] + one_ref[...]) + (two_ref[...] + three_ref[...])
    offset = lax.broadcasted_iota(jnp.int32, (1, 2 * BLOCK), 1)
    live = (label_ref[...] >= 0) & (offset < length_ref[0])
    total = jnp.where(live, total, 0.0).astype(BF16)
    row = lax.broadcasted_iota(jnp.int32, (32, BLOCK), 0)
    row_w = lax.broadcasted_iota(jnp.int32, (32, LANES), 0)
    over_first = (((0,), (0,)), ((), ()))
    terms = []
    for b in range(2):
        block = slice(b * BLOCK, (b + 1) * BLOCK)
        ranks = total[:, block]
        down = jnp.dot(ranks, attn_ref[block, :], preferred_element_type=F32)
        up = jnp.dot(ranks, grad_ref[block, :], preferred_element_type=F32)
        terms.append((down, up))
        shifted = pltpu.roll(ranks.astype(F32), 30, 0)
        outer = jnp.where((row & 2) == 0, shifted, 0.0).astype(BF16)
        back = lax.dot_general(outer, maps_ref[b * 32:(b + 1) * 32, :], over_first, preferred_element_type=F32)
        back_ref[block, :] = (adapter_scale * back).astype(BF16)
    for c in range(BANDS):
        band = slice(c * LANES, (c + 1) * LANES)
        both = [
            adapter_scale * jnp.where((row_w & 2) == 0, up[:, band], down[:, band])
            for down, up in terms
        ]
        for q in range(QUARTERS):
            pair = jnp.concatenate([one[q * 8:(q + 1) * 8] for one in both], axis=0)
            term_ref[c * 64 + q * 16:c * 64 + (q + 1) * 16, :] = pair.astype(BF16)


def add_up(in_ref, ids_ref, out_ref, in_f, ids_f):
    in_f[...] = in_ref[...].astype(F32)
    ids_f[...] = ids_ref[...].astype(F32)
    lane = lax.broadcasted_iota(jnp.int32, (PEERS, LANES), 1)
    over_first = (((0,), (0,)), ((), ()))
    total = jnp.zeros((LANES, 8 * LANES), F32)
    for b in range(2):
        which = ids_f[rows_of(4 + b, PEERS, 8), :].astype(jnp.int32)
        chosen = (lane == which).astype(F32).astype(BF16)
        terms = jnp.concatenate(
            [in_f[rows_of(b * 8 + k, PEERS, 16), :] for k in range(8)], axis=1
        ).astype(BF16)
        total += lax.dot_general(chosen, terms, over_first, preferred_element_type=F32)
    for k in range(8):
        out_ref[rows_of(k, 32, 8), :] = total[:32, k * LANES:(k + 1) * LANES]


def unpack(in_ref, down_ref, up_ref, rows_f):
    for m, map_ref in ((0, up_ref), (1, down_ref)):
        for i in range(2):
            rows_f[rows_of(i, PEERS, 2), :] = in_ref[rows_of(2 * m + i, PEERS, 4), :]
        for c in range(BANDS):
            map_ref[:, c * LANES:(c + 1) * LANES] = rows_f[c * 8:(c + 1) * 8, :]


def call(kernel, outs, specs, scratch=()):
    return pl.pallas_call(
        kernel,
        out_shape=[jax.ShapeDtypeStruct(shape, dtype) for shape, dtype in outs],
        in_specs=specs,
        out_specs=[VMEM] * len(outs),
        scratch_shapes=[pltpu.VMEM(shape, dtype) for shape, dtype in scratch],
        compiler_params=PARAMS,
    )


def swap(x):
    chunks = x.reshape(PEERS, x.shape[0] // PEERS, LANES)
    return lax.all_to_all(chunks, "dp", 0, 0, tiled=True).reshape(x.shape)


def from_peer(x, k):
    return lax.ppermute(x, "tensor", [(i, i ^ k) for i in range(4)])


def per_device(attn, output_gradient, down_weight, up_weight, adapter_of_row, lengths):
    width = attn.shape[1]
    me = lax.axis_index("tensor")
    slices = [
        lax.dynamic_slice_in_dim(output_gradient, (me ^ k) * width, width, 1) for k in range(4)
    ]
    pieces = [slices[0]] + [from_peer(slices[k], k) for k in (1, 2, 3)]

    (packed,) = call(
        pack_tables,
        [((8 * PEERS, LANES), BF16)],
        [VMEM, VMEM, SMEM],
        [((2 * PEERS, LANES), F32), ((8 * PEERS, LANES), F32)],
    )(down_weight, up_weight, adapter_of_row)
    tables = swap(packed)
    (picked,) = call(
        pick_rows,
        [((16 * PEERS, LANES), BF16)],
        [VMEM],
        [((8 * PEERS, LANES), F32), ((16 * PEERS, LANES), F32)],
    )(tables)
    picked = swap(picked)
    maps, grad, part = call(
        project,
        [((64, width), BF16), ((2 * BLOCK, width), BF16), ((32, 2 * BLOCK), F32)],
        [VMEM] * 6 + [SMEM],
    )(picked, attn, *pieces, me.astype(jnp.int32).reshape(1))
    parts = [part] + [from_peer(part, k) for k in (1, 2, 3)]
    attention_gradient, terms = call(
        expand,
        [((2 * BLOCK, width), BF16), ((16 * PEERS, LANES), BF16)],
        [VMEM] * 5 + [SMEM] + [VMEM] * 3,
    )(*parts, adapter_of_row.reshape(1, -1), lengths, maps, attn, grad)
    terms = swap(terms)
    (sums,) = call(
        add_up,
        [((4 * PEERS, LANES), F32)],
        [VMEM, VMEM],
        [((16 * PEERS, LANES), F32), ((8 * PEERS, LANES), F32)],
    )(terms, tables)
    sums = swap(sums)
    grad_a, grad_b = call(
        unpack, [((8, width), F32), ((8, width), F32)], [VMEM], [((2 * PEERS, LANES), F32)]
    )(sums)
    return attention_gradient, grad_a, grad_b


def solution(mesh):
    return jax.shard_map(
        per_device,
        mesh=mesh,
        in_specs=(
            P("dp", "tensor"),
            P(("dp", "tensor"), None),
            P("dp", "tensor"),
            P("dp", "tensor"),
            P("dp"),
            P("dp"),
        ),
        out_specs=(P("dp", "tensor"), P("dp", "tensor"), P("dp", "tensor")),
        check_vma=False,
    )
```

```python
import jax
import jax.numpy as jnp
from jax import lax
from jax.experimental import pallas as pl
from jax.experimental.pallas import tpu as pltpu
from jax.sharding import PartitionSpec as P

LANES = 128
BLOCK = 128
PEERS = 64
BANDS = 16
QUARTERS = 4

F32 = jnp.float32
BF16 = jnp.bfloat16

adapter_scale = 2.0

VMEM = pl.BlockSpec(memory_space=pltpu.VMEM)
ANY = pl.BlockSpec(memory_space=pl.ANY)
SMEM = pl.BlockSpec(memory_space=pltpu.SMEM)
PARAMS = pltpu.CompilerParams(vmem_limit_bytes=40 * 1024 * 1024)


def rows_of(first, size, stride):
    return pl.ds(first, size, stride=stride)


def pack_tables(
    down_hbm, up_hbm, label_hbm, length_hbm, out_ref, live_ref, down_ref, up_ref, label_ref, length_ref, rows_f, out_f, sems
):
    copies = [
        pltpu.make_async_copy(src, dst, sems.at[n])
        for n, (src, dst) in enumerate(
            ((label_hbm, label_ref), (length_hbm, length_ref), (down_hbm, down_ref), (up_hbm, up_ref))
        )
    ]
    for copy in copies:
        copy.start()
    for b in range(2):
        out_f[rows_of(6 + b, PEERS, 8), :] = jnp.zeros((PEERS, LANES), F32)
    copies[0].wait()
    labels = label_ref[...]
    for b in range(2):
        which = jnp.maximum(labels[b:b + 1, 0:1], 0).astype(F32)
        out_f[rows_of(4 + b, PEERS, 8), :] = jnp.broadcast_to(which, (PEERS, LANES))
    copies[1].wait()
    offset = lax.broadcasted_iota(jnp.int32, (2, BLOCK), 0) * BLOCK + lax.broadcasted_iota(jnp.int32, (2, BLOCK), 1)
    live_ref[...] = jnp.where((labels >= 0) & (offset < length_ref[0]), 1.0, 0.0)
    for m, map_ref in enumerate((down_ref, up_ref)):
        copies[2 + m].wait()
        for c in range(BANDS):
            rows_f[c * 8:(c + 1) * 8, :] = map_ref[:, c * LANES:(c + 1) * LANES].astype(F32)
        for i in range(2):
            out_f[rows_of(2 * m + i, PEERS, 8), :] = rows_f[rows_of(i, PEERS, 2), :]
    out_ref[...] = out_f[...].astype(BF16)


def pick_rows(in_ref, out_ref, in_f, out_f):
    in_f[...] = in_ref[...].astype(F32)
    table = jnp.concatenate([in_f[rows_of(k, PEERS, 8), :] for k in range(4)], axis=1).astype(BF16)
    lane = lax.broadcasted_iota(jnp.int32, (PEERS, LANES), 1)
    for b in range(2):
        which = in_f[rows_of(4 + b, PEERS, 8), :].astype(jnp.int32)
        for h in range(2):
            chosen = (lane == 2 * which + h).astype(F32).astype(BF16)[:, :PEERS]
            picked = jnp.dot(chosen, table, preferred_element_type=F32)
            for k in range(4):
                out_f[rows_of(b * 8 + h * 4 + k, PEERS, 16), :] = picked[:, k * LANES:(k + 1) * LANES]
    out_ref[...] = out_f[...].astype(BF16)


def project(picked_ref, attn_ref, own_ref, one_ref, two_ref, three_ref, place_ref, maps_ref, grad_ref, part_ref):
    me = place_ref[0]
    for k, piece in enumerate((own_ref, one_ref, two_ref, three_ref)):
        first = pl.multiple_of(lax.bitwise_xor(me, k) * 64, 64)
        grad_ref[pl.ds(first, 64), :] = piece[...]
    for c in range(BANDS):
        rows = picked_ref[c * 64:(c + 1) * 64, :].astype(F32).reshape(QUARTERS, 2, 8, LANES)
        for b in range(2):
            maps_ref[b * 32:(b + 1) * 32, c * LANES:(c + 1) * LANES] = rows[:, b].reshape(32, LANES).astype(BF16)
    row = lax.broadcasted_iota(jnp.int32, (32, BLOCK), 0)
    over_last = (((1,), (1,)), ((), ()))
    for b in range(2):
        maps = maps_ref[b * 32:(b + 1) * 32, :]
        block = slice(b * BLOCK, (b + 1) * BLOCK)
        inner = lax.dot_general(maps, attn_ref[block, :], over_last, preferred_element_type=F32)
        outer = lax.dot_general(maps, grad_ref[block, :], over_last, preferred_element_type=F32)
        part_ref[:, block] = jnp.where((row & 2) == 0, inner, outer)


def make_terms(own_ref, one_ref, two_ref, three_ref, live_ref, attn_ref, grad_ref, ranks_ref, term_ref):
    total = (own_ref[...] + one_ref[...]) + (two_ref[...] + three_ref[...])
    row = lax.broadcasted_iota(jnp.int32, (32, LANES), 0)
    terms = []
    for b in range(2):
        block = slice(b * BLOCK, (b + 1) * BLOCK)
        ranks = jnp.where(live_ref[b:b + 1, :] > 0, total[:, block], 0.0).astype(BF16)
        ranks_ref[:, block] = ranks
        down = jnp.dot(ranks, attn_ref[block, :], preferred_element_type=F32)
        up = jnp.dot(ranks, grad_ref[block, :], preferred_element_type=F32)
        terms.append((down, up))
    for c in range(BANDS):
        band = slice(c * LANES, (c + 1) * LANES)
        both = [
            adapter_scale * jnp.where((row & 2) == 0, up[:, band], down[:, band])
            for down, up in terms
        ]
        for q in range(QUARTERS):
            pair = jnp.concatenate([one[q * 8:(q + 1) * 8] for one in both], axis=0)
            term_ref[c * 64 + q * 16:c * 64 + (q + 1) * 16, :] = pair.astype(BF16)


def go_back(ranks_ref, maps_ref, back_ref):
    row = lax.broadcasted_iota(jnp.int32, (32, BLOCK), 0)
    over_first = (((0,), (0,)), ((), ()))
    for b in range(2):
        block = slice(b * BLOCK, (b + 1) * BLOCK)
        shifted = pltpu.roll(ranks_ref[:, block].astype(F32), 30, 0)
        outer = jnp.where((row & 2) == 0, shifted, 0.0).astype(BF16)
        back = lax.dot_general(outer, maps_ref[b * 32:(b + 1) * 32, :], over_first, preferred_element_type=F32)
        back_ref[block, :] = (adapter_scale * back).astype(BF16)


def add_up(in_ref, ids_ref, out_ref, in_f, ids_f):
    in_f[...] = in_ref[...].astype(F32)
    ids_f[...] = ids_ref[...].astype(F32)
    lane = lax.broadcasted_iota(jnp.int32, (PEERS, LANES), 1)
    over_first = (((0,), (0,)), ((), ()))
    total = jnp.zeros((LANES, 8 * LANES), F32)
    for b in range(2):
        which = ids_f[rows_of(4 + b, PEERS, 8), :].astype(jnp.int32)
        chosen = (lane == which).astype(F32).astype(BF16)
        terms = jnp.concatenate(
            [in_f[rows_of(b * 8 + k, PEERS, 16), :] for k in range(8)], axis=1
        ).astype(BF16)
        total += lax.dot_general(chosen, terms, over_first, preferred_element_type=F32)
    for k in range(8):
        out_ref[rows_of(k, 32, 8), :] = total[:32, k * LANES:(k + 1) * LANES]


def unpack(in_ref, down_ref, up_ref, rows_f):
    for m, map_ref in ((0, up_ref), (1, down_ref)):
        for i in range(2):
            rows_f[rows_of(i, PEERS, 2), :] = in_ref[rows_of(2 * m + i, PEERS, 4), :]
        for c in range(BANDS):
            map_ref[:, c * LANES:(c + 1) * LANES] = rows_f[c * 8:(c + 1) * 8, :]


def call(kernel, outs, specs, scratch=(), cost=None):
    return pl.pallas_call(
        kernel,
        out_shape=[jax.ShapeDtypeStruct(shape, dtype) for shape, dtype in outs],
        in_specs=specs,
        out_specs=[VMEM] * len(outs),
        scratch_shapes=scratch,
        compiler_params=PARAMS,
        cost_estimate=cost,
    )


def swap(x):
    chunks = x.reshape(PEERS, x.shape[0] // PEERS, LANES)
    return lax.all_to_all(chunks, "dp", 0, 0, tiled=True).reshape(x.shape)


def from_peer(x, k):
    return lax.ppermute(x, "tensor", [(i, i ^ k) for i in range(4)])


def per_device(attn, output_gradient, down_weight, up_weight, adapter_of_row, lengths):
    width = attn.shape[1]
    me = lax.axis_index("tensor")
    slices = [
        lax.dynamic_slice_in_dim(output_gradient, (me ^ k) * width, width, 1) for k in range(4)
    ]
    pieces = [slices[0]] + [from_peer(slices[k], k) for k in (1, 2, 3)]

    packed, live = call(
        pack_tables,
        [((8 * PEERS, LANES), BF16), ((2, BLOCK), F32)],
        [ANY] * 4,
        [
            pltpu.VMEM((8, width), BF16),
            pltpu.VMEM((8, width), BF16),
            pltpu.VMEM((2, BLOCK), jnp.int32),
            pltpu.SMEM((1,), jnp.int32),
            pltpu.VMEM((2 * PEERS, LANES), F32),
            pltpu.VMEM((8 * PEERS, LANES), F32),
            pltpu.SemaphoreType.DMA((4,)),
        ],
    )(down_weight, up_weight, adapter_of_row.reshape(2, BLOCK), lengths)
    tables = swap(packed)
    tables, pieces[1], pieces[3] = lax.optimization_barrier((tables, pieces[1], pieces[3]))
    (picked,) = call(
        pick_rows,
        [((16 * PEERS, LANES), BF16)],
        [VMEM],
        [pltpu.VMEM((8 * PEERS, LANES), F32), pltpu.VMEM((16 * PEERS, LANES), F32)],
    )(tables)
    picked = swap(picked)
    maps, grad, part = call(
        project,
        [((64, width), BF16), ((2 * BLOCK, width), BF16), ((32, 2 * BLOCK), F32)],
        [VMEM] * 6 + [SMEM],
    )(picked, attn, *pieces, me.astype(jnp.int32).reshape(1))
    parts = [part] + [from_peer(part, k) for k in (1, 2, 3)]
    ranks, terms = call(
        make_terms,
        [((32, 2 * BLOCK), BF16), ((16 * PEERS, LANES), BF16)],
        [VMEM] * 7,
    )(*parts, live, attn, grad)
    terms = swap(terms)
    (attention_gradient,) = call(
        go_back,
        [((2 * BLOCK, width), BF16)],
        [VMEM] * 2,
        cost=pl.CostEstimate(flops=2 * 32 * 256 * 2048, bytes_accessed=2 << 20, transcendentals=0),
    )(ranks, maps)
    (sums,) = call(
        add_up,
        [((4 * PEERS, LANES), F32)],
        [VMEM, VMEM],
        [pltpu.VMEM((16 * PEERS, LANES), F32), pltpu.VMEM((8 * PEERS, LANES), F32)],
    )(terms, tables)
    sums = swap(sums)
    grad_a, grad_b = call(
        unpack,
        [((8, width), F32), ((8, width), F32)],
        [VMEM],
        [pltpu.VMEM((2 * PEERS, LANES), F32)],
    )(sums)
    return attention_gradient, grad_a, grad_b


def solution(mesh):
    return jax.shard_map(
        per_device,
        mesh=mesh,
        in_specs=(
            P("dp", "tensor"),
            P(("dp", "tensor"), None),
            P("dp", "tensor"),
            P("dp", "tensor"),
            P("dp"),
            P("dp"),
        ),
        out_specs=(P("dp", "tensor"), P("dp", "tensor"), P("dp", "tensor")),
        check_vma=False,
    )
```

```python
import jax
import jax.numpy as jnp
from jax import lax
from jax.experimental import pallas as pl
from jax.experimental.pallas import tpu as pltpu
from jax.sharding import PartitionSpec as P

LANES = 128
BLOCK = 128
PEERS = 64
BANDS = 16
QUARTERS = 4

F32 = jnp.float32
BF16 = jnp.bfloat16

adapter_scale = 2.0

VMEM = pl.BlockSpec(memory_space=pltpu.VMEM)
ANY = pl.BlockSpec(memory_space=pl.ANY)
SMEM = pl.BlockSpec(memory_space=pltpu.SMEM)
MIB = 1024 * 1024


def rows_of(first, size, stride):
    return pl.ds(first, size, stride=stride)


def pack_tables(
    place_ref, down_hbm, up_hbm, label_hbm, length_hbm, grad_hbm,
    out_ref, own_ref, one_ref, two_ref, three_ref,
    down_ref, up_ref, label_ref, length_ref, rows_f, out_f, sems
):
    width = own_ref.shape[1]
    moves = [(label_hbm, label_ref), (length_hbm, length_ref), (down_hbm, down_ref), (up_hbm, up_ref)]
    for k, piece in ((3, three_ref), (2, two_ref), (1, one_ref), (0, own_ref)):
        first = pl.multiple_of(lax.bitwise_xor(place_ref[0], k) * width, width)
        moves.append((grad_hbm.at[:, pl.ds(first, width)], piece.at[pl.ds(0, 64), :]))
    copies = [pltpu.make_async_copy(src, dst, sems.at[n]) for n, (src, dst) in enumerate(moves)]
    for copy in copies:
        copy.start()
    for b in range(2):
        out_f[rows_of(6 + b, PEERS, 8), :] = jnp.zeros((PEERS, LANES), F32)
    copies[0].wait()
    labels = label_ref[...]
    for b in range(2):
        which = jnp.maximum(labels[b:b + 1, 0:1], 0).astype(F32)
        out_f[rows_of(4 + b, PEERS, 8), :] = jnp.broadcast_to(which, (PEERS, LANES))
    copies[1].wait()
    offset = lax.broadcasted_iota(jnp.int32, (2, BLOCK), 0) * BLOCK + lax.broadcasted_iota(jnp.int32, (2, BLOCK), 1)
    live = jnp.where((labels >= 0) & (offset < length_ref[0]), 1.0, 0.0)
    for b in range(2):
        rows = jnp.broadcast_to(live[b:b + 1, :], (16, BLOCK))
        own_ref[64:80, b * BLOCK:(b + 1) * BLOCK] = rows.astype(BF16)
    for m, map_ref in enumerate((down_ref, up_ref)):
        copies[2 + m].wait()
        for c in range(BANDS):
            rows_f[c * 8:(c + 1) * 8, :] = map_ref[:, c * LANES:(c + 1) * LANES].astype(F32)
        for i in range(2):
            out_f[rows_of(2 * m + i, PEERS, 8), :] = rows_f[rows_of(i, PEERS, 2), :]
    out_ref[...] = out_f[...].astype(BF16)
    for copy in copies[4:]:
        copy.wait()


def pick_rows(in_ref, out_ref, in_f, out_f):
    in_f[...] = in_ref[...].astype(F32)
    table = jnp.concatenate([in_f[rows_of(k, PEERS, 8), :] for k in range(4)], axis=1).astype(BF16)
    lane = lax.broadcasted_iota(jnp.int32, (PEERS, LANES), 1)
    for b in range(2):
        which = in_f[rows_of(4 + b, PEERS, 8), :].astype(jnp.int32)
        for h in range(2):
            chosen = (lane == 2 * which + h).astype(F32).astype(BF16)[:, :PEERS]
            picked = jnp.dot(chosen, table, preferred_element_type=F32)
            for k in range(4):
                out_f[rows_of(b * 8 + h * 4 + k, PEERS, 16), :] = picked[:, k * LANES:(k + 1) * LANES]
    out_ref[...] = out_f[...].astype(BF16)


def project(picked_ref, attn_ref, own_ref, one_ref, two_ref, three_ref, place_ref, maps_ref, grad_ref, part_ref):
    me = place_ref[0]
    for k, piece in enumerate((own_ref, one_ref, two_ref, three_ref)):
        first = pl.multiple_of(lax.bitwise_xor(me, k) * 64, 64)
        grad_ref[pl.ds(first, 64), :] = piece[:64, :]
    live = own_ref[64:80, :2 * BLOCK].astype(F32)[:1, :]
    for c in range(BANDS):
        rows = picked_ref[c * 64:(c + 1) * 64, :].astype(F32).reshape(QUARTERS, 2, 8, LANES)
        for b in range(2):
            maps_ref[b * 32:(b + 1) * 32, c * LANES:(c + 1) * LANES] = rows[:, b].reshape(32, LANES).astype(BF16)
    row = lax.broadcasted_iota(jnp.int32, (32, BLOCK), 0)
    over_last = (((1,), (1,)), ((), ()))
    for b in range(2):
        maps = maps_ref[b * 32:(b + 1) * 32, :]
        block = slice(b * BLOCK, (b + 1) * BLOCK)
        inner = lax.dot_general(maps, attn_ref[block, :], over_last, preferred_element_type=F32)
        outer = lax.dot_general(maps, grad_ref[block, :], over_last, preferred_element_type=F32)
        part_ref[:, block] = jnp.where(live[:, block] > 0, jnp.where((row & 2) == 0, inner, outer), 0.0)


def make_terms(own_ref, one_ref, two_ref, three_ref, attn_ref, grad_ref, ranks_ref, term_ref):
    total = (own_ref[...] + one_ref[...]) + (two_ref[...] + three_ref[...])
    row = lax.broadcasted_iota(jnp.int32, (32, LANES), 0)
    terms = []
    for b in range(2):
        block = slice(b * BLOCK, (b + 1) * BLOCK)
        ranks = total[:, block].astype(BF16)
        ranks_ref[:, block] = ranks
        down = jnp.dot(ranks, attn_ref[block, :], preferred_element_type=F32)
        up = jnp.dot(ranks, grad_ref[block, :], preferred_element_type=F32)
        terms.append((down, up))
    for c in range(BANDS):
        band = slice(c * LANES, (c + 1) * LANES)
        both = [
            adapter_scale * jnp.where((row & 2) == 0, up[:, band], down[:, band])
            for down, up in terms
        ]
        for q in range(QUARTERS):
            pair = jnp.concatenate([one[q * 8:(q + 1) * 8] for one in both], axis=0)
            term_ref[c * 64 + q * 16:c * 64 + (q + 1) * 16, :] = pair.astype(BF16)


def go_back(ranks_ref, maps_ref, back_ref):
    row = lax.broadcasted_iota(jnp.int32, (32, BLOCK), 0)
    over_first = (((0,), (0,)), ((), ()))
    for b in range(2):
        block = slice(b * BLOCK, (b + 1) * BLOCK)
        shifted = pltpu.roll(ranks_ref[:, block].astype(F32), 30, 0)
        outer = jnp.where((row & 2) == 0, shifted, 0.0).astype(BF16)
        back = lax.dot_general(outer, maps_ref[b * 32:(b + 1) * 32, :], over_first, preferred_element_type=F32)
        back_ref[block, :] = (adapter_scale * back).astype(BF16)


def add_up(in_ref, ids_ref, out_ref, in_f, ids_f):
    in_f[...] = in_ref[...].astype(F32)
    ids_f[...] = ids_ref[...].astype(F32)
    lane = lax.broadcasted_iota(jnp.int32, (PEERS, LANES), 1)
    over_first = (((0,), (0,)), ((), ()))
    total = jnp.zeros((LANES, 8 * LANES), F32)
    for b in range(2):
        which = ids_f[rows_of(4 + b, PEERS, 8), :].astype(jnp.int32)
        chosen = (lane == which).astype(F32).astype(BF16)
        terms = jnp.concatenate(
            [in_f[rows_of(b * 8 + k, PEERS, 16), :] for k in range(8)], axis=1
        ).astype(BF16)
        total += lax.dot_general(chosen, terms, over_first, preferred_element_type=F32)
    for k in range(8):
        out_ref[rows_of(k, 32, 8), :] = total[:32, k * LANES:(k + 1) * LANES]


def unpack(in_ref, down_ref, up_ref, rows_f):
    for m, map_ref in ((0, up_ref), (1, down_ref)):
        for i in range(2):
            rows_f[rows_of(i, PEERS, 2), :] = in_ref[rows_of(2 * m + i, PEERS, 4), :]
        for c in range(BANDS):
            map_ref[:, c * LANES:(c + 1) * LANES] = rows_f[c * 8:(c + 1) * 8, :]


def call(kernel, outs, specs, scratch=(), cost=None, limit=40 * MIB):
    return pl.pallas_call(
        kernel,
        out_shape=[jax.ShapeDtypeStruct(shape, dtype) for shape, dtype in outs],
        in_specs=specs,
        out_specs=[VMEM] * len(outs),
        scratch_shapes=scratch,
        compiler_params=pltpu.CompilerParams(vmem_limit_bytes=limit),
        cost_estimate=cost,
    )


def swap(x):
    chunks = x.reshape(PEERS, x.shape[0] // PEERS, LANES)
    return lax.all_to_all(chunks, "dp", 0, 0, tiled=True).reshape(x.shape)


def from_peer(x, k):
    return lax.ppermute(x, "tensor", [(i, i ^ k) for i in range(4)])


def per_device(attn, output_gradient, down_weight, up_weight, adapter_of_row, lengths):
    width = attn.shape[1]
    me = lax.axis_index("tensor")
    me = me.astype(jnp.int32).reshape(1)
    piece = ((64, width), BF16)
    packed, *pieces = call(
        pack_tables,
        [((8 * PEERS, LANES), BF16), ((80, width), BF16), piece, piece, piece],
        [SMEM] + [ANY] * 5,
        [
            pltpu.VMEM((8, width), BF16),
            pltpu.VMEM((8, width), BF16),
            pltpu.VMEM((2, BLOCK), jnp.int32),
            pltpu.SMEM((1,), jnp.int32),
            pltpu.VMEM((2 * PEERS, LANES), F32),
            pltpu.VMEM((8 * PEERS, LANES), F32),
            pltpu.SemaphoreType.DMA((8,)),
        ],
        limit=56 * MIB,
    )(me, down_weight, up_weight, adapter_of_row.reshape(2, BLOCK), lengths, output_gradient)
    pieces = [pieces[0]] + [from_peer(pieces[k], k) for k in (1, 2, 3)]
    tables = swap(packed)
    tables, *pieces = lax.optimization_barrier((tables, *pieces))
    (picked,) = call(
        pick_rows,
        [((16 * PEERS, LANES), BF16)],
        [VMEM],
        [pltpu.VMEM((8 * PEERS, LANES), F32), pltpu.VMEM((16 * PEERS, LANES), F32)],
    )(tables)
    picked = swap(picked)
    maps, grad, part = call(
        project,
        [((64, width), BF16), ((2 * BLOCK, width), BF16), ((32, 2 * BLOCK), F32)],
        [VMEM] * 6 + [SMEM],
    )(picked, attn, *pieces, me)
    parts = [part] + [from_peer(part, k) for k in (1, 2, 3)]
    ranks, terms = call(
        make_terms,
        [((32, 2 * BLOCK), BF16), ((16 * PEERS, LANES), BF16)],
        [VMEM] * 6,
    )(*parts, attn, grad)
    terms = swap(terms)
    (attention_gradient,) = call(
        go_back,
        [((2 * BLOCK, width), BF16)],
        [VMEM] * 2,
        cost=pl.CostEstimate(flops=2 * 32 * 256 * 2048, bytes_accessed=2 << 20, transcendentals=0),
    )(ranks, maps)
    (sums,) = call(
        add_up,
        [((4 * PEERS, LANES), F32)],
        [VMEM, VMEM],
        [pltpu.VMEM((16 * PEERS, LANES), F32), pltpu.VMEM((8 * PEERS, LANES), F32)],
    )(terms, tables)
    sums = swap(sums)
    grad_a, grad_b = call(
        unpack,
        [((8, width), F32), ((8, width), F32)],
        [VMEM],
        [pltpu.VMEM((2 * PEERS, LANES), F32)],
    )(sums)
    return attention_gradient, grad_a, grad_b


def solution(mesh):
    return jax.shard_map(
        per_device,
        mesh=mesh,
        in_specs=(
            P("dp", "tensor"),
            P(("dp", "tensor"), None),
            P("dp", "tensor"),
            P("dp", "tensor"),
            P("dp"),
            P("dp"),
        ),
        out_specs=(P("dp", "tensor"), P("dp", "tensor"), P("dp", "tensor")),
        check_vma=False,
    )
```

```python
import jax
import jax.numpy as jnp
from jax import lax
from jax.experimental import pallas as pl
from jax.experimental.pallas import tpu as pltpu
from jax.sharding import PartitionSpec as P

LANES = 128
BLOCK = 128
PEERS = 64
BANDS = 16
QUARTERS = 4

F32 = jnp.float32
BF16 = jnp.bfloat16

adapter_scale = 2.0

VMEM = pl.BlockSpec(memory_space=pltpu.VMEM)
ANY = pl.BlockSpec(memory_space=pl.ANY)
SMEM = pl.BlockSpec(memory_space=pltpu.SMEM)
MIB = 1024 * 1024


def rows_of(first, size, stride):
    return pl.ds(first, size, stride=stride)


def pack_tables(down_hbm, up_hbm, label_hbm, out_ref, down_ref, up_ref, label_ref, rows_f, out_f, sems):
    moves = ((label_hbm, label_ref), (down_hbm, down_ref), (up_hbm, up_ref))
    copies = [pltpu.make_async_copy(src, dst, sems.at[n]) for n, (src, dst) in enumerate(moves)]
    for copy in copies:
        copy.start()
    for b in range(2):
        out_f[rows_of(6 + b, PEERS, 8), :] = jnp.zeros((PEERS, LANES), F32)
    copies[0].wait()
    labels = label_ref[...]
    for b in range(2):
        which = jnp.maximum(labels[b:b + 1, 0:1], 0).astype(F32)
        out_f[rows_of(4 + b, PEERS, 8), :] = jnp.broadcast_to(which, (PEERS, LANES))
    for m, map_ref in enumerate((down_ref, up_ref)):
        copies[1 + m].wait()
        for c in range(BANDS):
            rows_f[c * 8:(c + 1) * 8, :] = map_ref[:, c * LANES:(c + 1) * LANES].astype(F32)
        for i in range(2):
            out_f[rows_of(2 * m + i, PEERS, 8), :] = rows_f[rows_of(i, PEERS, 2), :]
    out_ref[...] = out_f[...].astype(BF16)


def pick_rows(in_ref, out_ref, in_f, out_f):
    in_f[...] = in_ref[...].astype(F32)
    table = jnp.concatenate([in_f[rows_of(k, PEERS, 8), :] for k in range(4)], axis=1).astype(BF16)
    lane = lax.broadcasted_iota(jnp.int32, (PEERS, LANES), 1)
    for b in range(2):
        which = in_f[rows_of(4 + b, PEERS, 8), :].astype(jnp.int32)
        for h in range(2):
            chosen = (lane == 2 * which + h).astype(F32).astype(BF16)[:, :PEERS]
            picked = jnp.dot(chosen, table, preferred_element_type=F32)
            for k in range(4):
                out_f[rows_of(b * 8 + h * 4 + k, PEERS, 16), :] = picked[:, k * LANES:(k + 1) * LANES]
    out_ref[...] = out_f[...].astype(BF16)


def project(
    place_ref, picked_ref, attn_ref, tokens_hbm, live_ref, maps_ref, grad_ref, part_ref, sem
):
    width = grad_ref.shape[1]
    first = pl.multiple_of(place_ref[0] * width, width)
    copy = pltpu.make_async_copy(tokens_hbm.at[:, pl.ds(first, width)], grad_ref, sem)
    copy.start()
    for c in range(BANDS):
        rows = picked_ref[c * 64:(c + 1) * 64, :].astype(F32).reshape(QUARTERS, 2, 8, LANES)
        for b in range(2):
            maps_ref[b * 32:(b + 1) * 32, c * LANES:(c + 1) * LANES] = rows[:, b].reshape(32, LANES).astype(BF16)
    copy.wait()
    row = lax.broadcasted_iota(jnp.int32, (32, BLOCK), 0)
    over_last = (((1,), (1,)), ((), ()))
    for b in range(2):
        maps = maps_ref[b * 32:(b + 1) * 32, :]
        block = slice(b * BLOCK, (b + 1) * BLOCK)
        inner = lax.dot_general(maps, attn_ref[block, :], over_last, preferred_element_type=F32)
        outer = lax.dot_general(maps, grad_ref[block, :], over_last, preferred_element_type=F32)
        part_ref[:, block] = jnp.where(live_ref[b:b + 1, :] > 0, jnp.where((row & 2) == 0, inner, outer), 0.0)


def make_terms(own_ref, one_ref, two_ref, three_ref, attn_ref, grad_ref, ranks_ref, term_ref):
    total = (own_ref[...] + one_ref[...]) + (two_ref[...] + three_ref[...])
    row = lax.broadcasted_iota(jnp.int32, (32, LANES), 0)
    terms = []
    for b in range(2):
        block = slice(b * BLOCK, (b + 1) * BLOCK)
        ranks = total[:, block].astype(BF16)
        ranks_ref[:, block] = ranks
        down = jnp.dot(ranks, attn_ref[block, :], preferred_element_type=F32)
        up = jnp.dot(ranks, grad_ref[block, :], preferred_element_type=F32)
        terms.append((down, up))
    for c in range(BANDS):
        band = slice(c * LANES, (c + 1) * LANES)
        both = [
            adapter_scale * jnp.where((row & 2) == 0, up[:, band], down[:, band])
            for down, up in terms
        ]
        for q in range(QUARTERS):
            pair = jnp.concatenate([one[q * 8:(q + 1) * 8] for one in both], axis=0)
            term_ref[c * 64 + q * 16:c * 64 + (q + 1) * 16, :] = pair.astype(BF16)


def go_back(ranks_ref, maps_ref, back_ref):
    row = lax.broadcasted_iota(jnp.int32, (32, BLOCK), 0)
    over_first = (((0,), (0,)), ((), ()))
    for b in range(2):
        block = slice(b * BLOCK, (b + 1) * BLOCK)
        shifted = pltpu.roll(ranks_ref[:, block].astype(F32), 30, 0)
        outer = jnp.where((row & 2) == 0, shifted, 0.0).astype(BF16)
        back = lax.dot_general(outer, maps_ref[b * 32:(b + 1) * 32, :], over_first, preferred_element_type=F32)
        back_ref[block, :] = (adapter_scale * back).astype(BF16)


def add_up(in_ref, ids_ref, out_ref, in_f, ids_f):
    in_f[...] = in_ref[...].astype(F32)
    ids_f[...] = ids_ref[...].astype(F32)
    lane = lax.broadcasted_iota(jnp.int32, (PEERS, LANES), 1)
    over_first = (((0,), (0,)), ((), ()))
    total = jnp.zeros((LANES, 8 * LANES), F32)
    for b in range(2):
        which = ids_f[rows_of(4 + b, PEERS, 8), :].astype(jnp.int32)
        chosen = (lane == which).astype(F32).astype(BF16)
        terms = jnp.concatenate(
            [in_f[rows_of(b * 8 + k, PEERS, 16), :] for k in range(8)], axis=1
        ).astype(BF16)
        total += lax.dot_general(chosen, terms, over_first, preferred_element_type=F32)
    for k in range(8):
        out_ref[rows_of(k, 32, 8), :] = total[:32, k * LANES:(k + 1) * LANES]


def unpack(in_ref, down_ref, up_ref, rows_f):
    for m, map_ref in ((0, up_ref), (1, down_ref)):
        for i in range(2):
            rows_f[rows_of(i, PEERS, 2), :] = in_ref[rows_of(2 * m + i, PEERS, 4), :]
        for c in range(BANDS):
            map_ref[:, c * LANES:(c + 1) * LANES] = rows_f[c * 8:(c + 1) * 8, :]


def call(kernel, outs, specs, scratch=(), cost=None, limit=40 * MIB):
    return pl.pallas_call(
        kernel,
        out_shape=[jax.ShapeDtypeStruct(shape, dtype) for shape, dtype in outs],
        in_specs=specs,
        out_specs=[VMEM] * len(outs),
        scratch_shapes=scratch,
        compiler_params=pltpu.CompilerParams(vmem_limit_bytes=limit),
        cost_estimate=cost,
    )


def swap(x):
    chunks = x.reshape(PEERS, x.shape[0] // PEERS, LANES)
    return lax.all_to_all(chunks, "dp", 0, 0, tiled=True).reshape(x.shape)


def from_peer(x, k):
    return lax.ppermute(x, "tensor", [(i, i ^ k) for i in range(4)])


def per_device(attn, output_gradient, down_weight, up_weight, adapter_of_row, lengths):
    width = attn.shape[1]
    me = lax.axis_index("tensor")
    me = me.astype(jnp.int32).reshape(1)
    labels = adapter_of_row.reshape(2, BLOCK)
    tokens = lax.all_gather(output_gradient, "tensor", axis=0, tiled=True)
    (packed,) = call(
        pack_tables,
        [((8 * PEERS, LANES), BF16)],
        [ANY] * 3,
        [
            pltpu.VMEM((8, width), BF16),
            pltpu.VMEM((8, width), BF16),
            pltpu.VMEM((2, BLOCK), jnp.int32),
            pltpu.VMEM((2 * PEERS, LANES), F32),
            pltpu.VMEM((8 * PEERS, LANES), F32),
            pltpu.SemaphoreType.DMA((3,)),
        ],
        limit=56 * MIB,
    )(down_weight, up_weight, labels)
    live = (adapter_of_row >= 0) & (jnp.arange(2 * BLOCK, dtype=jnp.int32) < lengths[0])
    live = live.astype(F32).reshape(2, BLOCK)
    tables, me, live = lax.optimization_barrier((swap(packed), me, live))
    (picked,) = call(
        pick_rows,
        [((16 * PEERS, LANES), BF16)],
        [VMEM],
        [pltpu.VMEM((8 * PEERS, LANES), F32), pltpu.VMEM((16 * PEERS, LANES), F32)],
    )(tables)
    picked = swap(picked)
    maps, grad, part = call(
        project,
        [((64, width), BF16), ((2 * BLOCK, width), BF16), ((32, 2 * BLOCK), F32)],
        [SMEM, VMEM, VMEM, ANY, VMEM],
        [pltpu.SemaphoreType.DMA(())],
        limit=52 * MIB,
    )(me, picked, attn, tokens, live)
    parts = [part] + [from_peer(part, k) for k in (1, 2, 3)]
    ranks, terms = call(
        make_terms,
        [((32, 2 * BLOCK), BF16), ((16 * PEERS, LANES), BF16)],
        [VMEM] * 6,
    )(*parts, attn, grad)
    terms = swap(terms)
    (attention_gradient,) = call(
        go_back,
        [((2 * BLOCK, width), BF16)],
        [VMEM] * 2,
        cost=pl.CostEstimate(flops=2 * 32 * 256 * 2048, bytes_accessed=2 << 20, transcendentals=0),
    )(ranks, maps)
    (sums,) = call(
        add_up,
        [((4 * PEERS, LANES), F32)],
        [VMEM, VMEM],
        [pltpu.VMEM((16 * PEERS, LANES), F32), pltpu.VMEM((8 * PEERS, LANES), F32)],
    )(terms, tables)
    sums = swap(sums)
    grad_a, grad_b = call(
        unpack,
        [((8, width), F32), ((8, width), F32)],
        [VMEM],
        [pltpu.VMEM((2 * PEERS, LANES), F32)],
    )(sums)
    return attention_gradient, grad_a, grad_b


def solution(mesh):
    return jax.shard_map(
        per_device,
        mesh=mesh,
        in_specs=(
            P("dp", "tensor"),
            P(("dp", "tensor"), None),
            P("dp", "tensor"),
            P("dp", "tensor"),
            P("dp"),
            P("dp"),
        ),
        out_specs=(P("dp", "tensor"), P("dp", "tensor"), P("dp", "tensor")),
        check_vma=False,
    )
```

```python
import functools

import jax
import jax.numpy as jnp
from jax import lax
from jax.experimental import pallas as pl
from jax.experimental.pallas import tpu as pltpu
from jax.sharding import PartitionSpec as P

LANES = 128
BLOCK = 128
PEERS = 64
BANDS = 16
QUARTERS = 4

F32 = jnp.float32
BF16 = jnp.bfloat16

adapter_scale = 2.0

VMEM = pl.BlockSpec(memory_space=pltpu.VMEM)
ANY = pl.BlockSpec(memory_space=pl.ANY)
SMEM = pl.BlockSpec(memory_space=pltpu.SMEM)
MIB = 1024 * 1024


def rows_of(first, size, stride):
    return pl.ds(first, size, stride=stride)


def pack_tables(down_hbm, up_hbm, label_hbm, out_ref, down_ref, up_ref, label_ref, rows_f, out_f, sems):
    moves = ((label_hbm, label_ref), (down_hbm, down_ref), (up_hbm, up_ref))
    copies = [pltpu.make_async_copy(src, dst, sems.at[n]) for n, (src, dst) in enumerate(moves)]
    for copy in copies:
        copy.start()
    for b in range(2):
        out_f[rows_of(6 + b, PEERS, 8), :] = jnp.zeros((PEERS, LANES), F32)
    copies[0].wait()
    labels = label_ref[...]
    for b in range(2):
        which = jnp.maximum(labels[b:b + 1, 0:1], 0).astype(F32)
        out_f[rows_of(4 + b, PEERS, 8), :] = jnp.broadcast_to(which, (PEERS, LANES))
    for m, map_ref in enumerate((down_ref, up_ref)):
        copies[1 + m].wait()
        for c in range(BANDS):
            rows_f[c * 8:(c + 1) * 8, :] = map_ref[:, c * LANES:(c + 1) * LANES].astype(F32)
        for i in range(2):
            out_f[rows_of(2 * m + i, PEERS, 8), :] = rows_f[rows_of(i, PEERS, 2), :]
    out_ref[...] = out_f[...].astype(BF16)


def cut_tokens(ks, place_ref, grad_hbm, packed_hbm, *refs):
    pieces, sems = refs[:-1], refs[-1]
    width = pieces[0].shape[1]
    copies = []
    for n, (k, piece) in enumerate(zip(ks, pieces)):
        first = pl.multiple_of(lax.bitwise_xor(place_ref[0], k) * width, width)
        copies.append(pltpu.make_async_copy(grad_hbm.at[:, pl.ds(first, width)], piece, sems.at[n]))
    for copy in copies:
        copy.start()
    for copy in copies:
        copy.wait()


def pick_rows(in_ref, out_ref, in_f, out_f):
    in_f[...] = in_ref[...].astype(F32)
    table = jnp.concatenate([in_f[rows_of(k, PEERS, 8), :] for k in range(4)], axis=1).astype(BF16)
    lane = lax.broadcasted_iota(jnp.int32, (PEERS, LANES), 1)
    for b in range(2):
        which = in_f[rows_of(4 + b, PEERS, 8), :].astype(jnp.int32)
        for h in range(2):
            chosen = (lane == 2 * which + h).astype(F32).astype(BF16)[:, :PEERS]
            picked = jnp.dot(chosen, table, preferred_element_type=F32)
            for k in range(4):
                out_f[rows_of(b * 8 + h * 4 + k, PEERS, 16), :] = picked[:, k * LANES:(k + 1) * LANES]
    out_ref[...] = out_f[...].astype(BF16)


def project(picked_ref, attn_ref, own_ref, one_ref, two_ref, three_ref, place_ref, live_ref, maps_ref, grad_ref, part_ref):
    me = place_ref[0]
    for k, piece in enumerate((own_ref, one_ref, two_ref, three_ref)):
        first = pl.multiple_of(lax.bitwise_xor(me, k) * 64, 64)
        grad_ref[pl.ds(first, 64), :] = piece[...]
    for c in range(BANDS):
        rows = picked_ref[c * 64:(c + 1) * 64, :].astype(F32).reshape(QUARTERS, 2, 8, LANES)
        for b in range(2):
            maps_ref[b * 32:(b + 1) * 32, c * LANES:(c + 1) * LANES] = rows[:, b].reshape(32, LANES).astype(BF16)
    row = lax.broadcasted_iota(jnp.int32, (32, BLOCK), 0)
    over_last = (((1,), (1,)), ((), ()))
    for b in range(2):
        maps = maps_ref[b * 32:(b + 1) * 32, :]
        block = slice(b * BLOCK, (b + 1) * BLOCK)
        inner = lax.dot_general(maps, attn_ref[block, :], over_last, preferred_element_type=F32)
        outer = lax.dot_general(maps, grad_ref[block, :], over_last, preferred_element_type=F32)
        part_ref[:, block] = jnp.where(live_ref[b:b + 1, :] > 0, jnp.where((row & 2) == 0, inner, outer), 0.0)


def make_terms(own_ref, one_ref, two_ref, three_ref, attn_ref, grad_ref, ranks_ref, term_ref):
    total = (own_ref[...] + one_ref[...]) + (two_ref[...] + three_ref[...])
    row = lax.broadcasted_iota(jnp.int32, (32, LANES), 0)
    terms = []
    for b in range(2):
        block = slice(b * BLOCK, (b + 1) * BLOCK)
        ranks = total[:, block].astype(BF16)
        ranks_ref[:, block] = ranks
        down = jnp.dot(ranks, attn_ref[block, :], preferred_element_type=F32)
        up = jnp.dot(ranks, grad_ref[block, :], preferred_element_type=F32)
        terms.append((down, up))
    for c in range(BANDS):
        band = slice(c * LANES, (c + 1) * LANES)
        both = [
            adapter_scale * jnp.where((row & 2) == 0, up[:, band], down[:, band])
            for down, up in terms
        ]
        for q in range(QUARTERS):
            pair = jnp.concatenate([one[q * 8:(q + 1) * 8] for one in both], axis=0)
            term_ref[c * 64 + q * 16:c * 64 + (q + 1) * 16, :] = pair.astype(BF16)


def go_back(ranks_ref, maps_ref, back_ref):
    row = lax.broadcasted_iota(jnp.int32, (32, BLOCK), 0)
    over_first = (((0,), (0,)), ((), ()))
    for b in range(2):
        block = slice(b * BLOCK, (b + 1) * BLOCK)
        shifted = pltpu.roll(ranks_ref[:, block].astype(F32), 30, 0)
        outer = jnp.where((row & 2) == 0, shifted, 0.0).astype(BF16)
        back = lax.dot_general(outer, maps_ref[b * 32:(b + 1) * 32, :], over_first, preferred_element_type=F32)
        back_ref[block, :] = (adapter_scale * back).astype(BF16)


def add_up(in_ref, ids_ref, out_ref, in_f, ids_f):
    in_f[...] = in_ref[...].astype(F32)
    ids_f[...] = ids_ref[...].astype(F32)
    lane = lax.broadcasted_iota(jnp.int32, (PEERS, LANES), 1)
    over_first = (((0,), (0,)), ((), ()))
    total = jnp.zeros((LANES, 8 * LANES), F32)
    for b in range(2):
        which = ids_f[rows_of(4 + b, PEERS, 8), :].astype(jnp.int32)
        chosen = (lane == which).astype(F32).astype(BF16)
        terms = jnp.concatenate(
            [in_f[rows_of(b * 8 + k, PEERS, 16), :] for k in range(8)], axis=1
        ).astype(BF16)
        total += lax.dot_general(chosen, terms, over_first, preferred_element_type=F32)
    for k in range(8):
        out_ref[rows_of(k, 32, 8), :] = total[:32, k * LANES:(k + 1) * LANES]


def unpack(in_ref, down_ref, up_ref, rows_f):
    for m, map_ref in ((0, up_ref), (1, down_ref)):
        for i in range(2):
            rows_f[rows_of(i, PEERS, 2), :] = in_ref[rows_of(2 * m + i, PEERS, 4), :]
        for c in range(BANDS):
            map_ref[:, c * LANES:(c + 1) * LANES] = rows_f[c * 8:(c + 1) * 8, :]


def call(kernel, outs, specs, scratch=(), cost=None, limit=40 * MIB):
    return pl.pallas_call(
        kernel,
        out_shape=[jax.ShapeDtypeStruct(shape, dtype) for shape, dtype in outs],
        in_specs=specs,
        out_specs=[VMEM] * len(outs),
        scratch_shapes=scratch,
        compiler_params=pltpu.CompilerParams(vmem_limit_bytes=limit),
        cost_estimate=cost,
    )


def swap(x):
    chunks = x.reshape(PEERS, x.shape[0] // PEERS, LANES)
    return lax.all_to_all(chunks, "dp", 0, 0, tiled=True).reshape(x.shape)


def from_peer(x, k):
    return lax.ppermute(x, "tensor", [(i, i ^ k) for i in range(4)])


def per_device(attn, output_gradient, down_weight, up_weight, adapter_of_row, lengths):
    width = attn.shape[1]
    me = lax.axis_index("tensor")
    me = me.astype(jnp.int32).reshape(1)
    (packed,) = call(
        pack_tables,
        [((8 * PEERS, LANES), BF16)],
        [ANY] * 3,
        [
            pltpu.VMEM((8, width), BF16),
            pltpu.VMEM((8, width), BF16),
            pltpu.VMEM((2, BLOCK), jnp.int32),
            pltpu.VMEM((2 * PEERS, LANES), F32),
            pltpu.VMEM((8 * PEERS, LANES), F32),
            pltpu.SemaphoreType.DMA((3,)),
        ],
        limit=56 * MIB,
    )(down_weight, up_weight, adapter_of_row.reshape(2, BLOCK))

    def cut(ks, flops):
        return call(
            functools.partial(cut_tokens, ks),
            [((64, width), BF16)] * len(ks),
            [SMEM, ANY, ANY],
            [pltpu.SemaphoreType.DMA((len(ks),))],
            cost=pl.CostEstimate(flops=flops, bytes_accessed=len(ks) << 19, transcendentals=0),
            limit=56 * MIB,
        )(me, output_gradient, packed)

    live = (adapter_of_row >= 0) & (jnp.arange(2 * BLOCK, dtype=jnp.int32) < lengths[0])
    live = live.astype(F32).reshape(2, BLOCK)
    one, three = cut((1, 3), 1000)
    own, two = cut((0, 2), 10 ** 10)
    one, three = from_peer(one, 1), from_peer(three, 3)
    tables = swap(packed)
    tables, live, own, two, one, three = lax.optimization_barrier((tables, live, own, two, one, three))
    pieces = [own, one, from_peer(two, 2), three]
    (picked,) = call(
        pick_rows,
        [((16 * PEERS, LANES), BF16)],
        [VMEM],
        [pltpu.VMEM((8 * PEERS, LANES), F32), pltpu.VMEM((16 * PEERS, LANES), F32)],
    )(tables)
    picked = swap(picked)
    maps, grad, part = call(
        project,
        [((64, width), BF16), ((2 * BLOCK, width), BF16), ((32, 2 * BLOCK), F32)],
        [VMEM] * 6 + [SMEM, VMEM],
    )(picked, attn, *pieces, me, live)
    parts = [part] + [from_peer(part, k) for k in (1, 2, 3)]
    ranks, terms = call(
        make_terms,
        [((32, 2 * BLOCK), BF16), ((16 * PEERS, LANES), BF16)],
        [VMEM] * 6,
    )(*parts, attn, grad)
    terms = swap(terms)
    (attention_gradient,) = call(
        go_back,
        [((2 * BLOCK, width), BF16)],
        [VMEM] * 2,
        cost=pl.CostEstimate(flops=2 * 32 * 256 * 2048, bytes_accessed=2 << 20, transcendentals=0),
    )(ranks, maps)
    (sums,) = call(
        add_up,
        [((4 * PEERS, LANES), F32)],
        [VMEM, VMEM],
        [pltpu.VMEM((16 * PEERS, LANES), F32), pltpu.VMEM((8 * PEERS, LANES), F32)],
    )(terms, tables)
    sums = swap(sums)
    grad_a, grad_b = call(
        unpack,
        [((8, width), F32), ((8, width), F32)],
        [VMEM],
        [pltpu.VMEM((2 * PEERS, LANES), F32)],
    )(sums)
    return attention_gradient, grad_a, grad_b


def solution(mesh):
    return jax.shard_map(
        per_device,
        mesh=mesh,
        in_specs=(
            P("dp", "tensor"),
            P(("dp", "tensor"), None),
            P("dp", "tensor"),
            P("dp", "tensor"),
            P("dp"),
            P("dp"),
        ),
        out_specs=(P("dp", "tensor"), P("dp", "tensor"), P("dp", "tensor")),
        check_vma=False,
    )
```

```python
import jax
import jax.numpy as jnp
from jax import lax
from jax.experimental import pallas as pl
from jax.experimental.pallas import tpu as pltpu
from jax.sharding import PartitionSpec as P

LANES = 128
BLOCK = 128
PEERS = 64
BANDS = 16
QUARTERS = 4

F32 = jnp.float32
BF16 = jnp.bfloat16

adapter_scale = 2.0

VMEM = pl.BlockSpec(memory_space=pltpu.VMEM)
ANY = pl.BlockSpec(memory_space=pl.ANY)
SMEM = pl.BlockSpec(memory_space=pltpu.SMEM)
MIB = 1024 * 1024


def rows_of(first, size, stride):
    return pl.ds(first, size, stride=stride)


def pack_tables(
    place_ref, down_hbm, up_hbm, label_hbm, grad_hbm,
    out_ref, near_ref, far_ref, down_ref, up_ref, label_ref, rows_f, out_f, sems
):
    width = near_ref.shape[1]
    moves = [(label_hbm, label_ref), (down_hbm, down_ref), (up_hbm, up_ref)]
    for k, piece in ((1, near_ref), (2, far_ref.at[pl.ds(0, 64), :]), (3, far_ref.at[pl.ds(64, 64), :])):
        first = pl.multiple_of(lax.bitwise_xor(place_ref[0], k) * width, width)
        moves.append((grad_hbm.at[:, pl.ds(first, width)], piece))
    copies = [pltpu.make_async_copy(src, dst, sems.at[n]) for n, (src, dst) in enumerate(moves)]
    for copy in copies:
        copy.start()
    for b in range(2):
        out_f[rows_of(6 + b, PEERS, 8), :] = jnp.zeros((PEERS, LANES), F32)
    copies[0].wait()
    labels = label_ref[...]
    for b in range(2):
        which = jnp.maximum(labels[b:b + 1, 0:1], 0).astype(F32)
        out_f[rows_of(4 + b, PEERS, 8), :] = jnp.broadcast_to(which, (PEERS, LANES))
    for m, map_ref in enumerate((down_ref, up_ref)):
        copies[1 + m].wait()
        for c in range(BANDS):
            rows_f[c * 8:(c + 1) * 8, :] = map_ref[:, c * LANES:(c + 1) * LANES].astype(F32)
        for i in range(2):
            out_f[rows_of(2 * m + i, PEERS, 8), :] = rows_f[rows_of(i, PEERS, 2), :]
    out_ref[...] = out_f[...].astype(BF16)
    for copy in copies[3:]:
        copy.wait()


def pick_rows(in_ref, out_ref, in_f, out_f):
    in_f[...] = in_ref[...].astype(F32)
    table = jnp.concatenate([in_f[rows_of(k, PEERS, 8), :] for k in range(4)], axis=1).astype(BF16)
    lane = lax.broadcasted_iota(jnp.int32, (PEERS, LANES), 1)
    for b in range(2):
        which = in_f[rows_of(4 + b, PEERS, 8), :].astype(jnp.int32)
        for h in range(2):
            chosen = (lane == 2 * which + h).astype(F32).astype(BF16)[:, :PEERS]
            picked = jnp.dot(chosen, table, preferred_element_type=F32)
            for k in range(4):
                out_f[rows_of(b * 8 + h * 4 + k, PEERS, 16), :] = picked[:, k * LANES:(k + 1) * LANES]
    out_ref[...] = out_f[...].astype(BF16)


def project(place_ref, picked_ref, attn_ref, tokens_hbm, one_ref, two_ref, three_ref, maps_ref, grad_ref, part_ref, sem):
    me = place_ref[0]
    width = grad_ref.shape[1]
    own = tokens_hbm.at[:, pl.ds(pl.multiple_of(me * width, width), width)]
    copy = pltpu.make_async_copy(own, grad_ref.at[pl.ds(pl.multiple_of(me * 64, 64), 64), :], sem)
    copy.start()
    for k, piece in ((1, one_ref), (2, two_ref), (3, three_ref)):
        first = pl.multiple_of(lax.bitwise_xor(me, k) * 64, 64)
        grad_ref[pl.ds(first, 64), :] = piece[:64, :]
    for c in range(BANDS):
        rows = picked_ref[c * 64:(c + 1) * 64, :].astype(F32).reshape(QUARTERS, 2, 8, LANES)
        for b in range(2):
            maps_ref[b * 32:(b + 1) * 32, c * LANES:(c + 1) * LANES] = rows[:, b].reshape(32, LANES).astype(BF16)
    copy.wait()
    row = lax.broadcasted_iota(jnp.int32, (32, BLOCK), 0)
    over_last = (((1,), (1,)), ((), ()))
    for b in range(2):
        maps = maps_ref[b * 32:(b + 1) * 32, :]
        block = slice(b * BLOCK, (b + 1) * BLOCK)
        inner = lax.dot_general(maps, attn_ref[block, :], over_last, preferred_element_type=F32)
        outer = lax.dot_general(maps, grad_ref[block, :], over_last, preferred_element_type=F32)
        part_ref[:, block] = jnp.where((row & 2) == 0, inner, outer)


def make_terms(own_ref, one_ref, two_ref, three_ref, live_ref, attn_ref, grad_ref, ranks_ref, term_ref):
    total = (own_ref[...] + one_ref[...]) + (two_ref[...] + three_ref[...])
    row = lax.broadcasted_iota(jnp.int32, (32, LANES), 0)
    terms = []
    for b in range(2):
        block = slice(b * BLOCK, (b + 1) * BLOCK)
        ranks = jnp.where(live_ref[b:b + 1, :] > 0, total[:, block], 0.0).astype(BF16)
        ranks_ref[:, block] = ranks
        down = jnp.dot(ranks, attn_ref[block, :], preferred_element_type=F32)
        up = jnp.dot(ranks, grad_ref[block, :], preferred_element_type=F32)
        terms.append((down, up))
    for c in range(BANDS):
        band = slice(c * LANES, (c + 1) * LANES)
        both = [
            adapter_scale * jnp.where((row & 2) == 0, up[:, band], down[:, band])
            for down, up in terms
        ]
        for q in range(QUARTERS):
            pair = jnp.concatenate([one[q * 8:(q + 1) * 8] for one in both], axis=0)
            term_ref[c * 64 + q * 16:c * 64 + (q + 1) * 16, :] = pair.astype(BF16)


def go_back(ranks_ref, maps_ref, back_ref):
    row = lax.broadcasted_iota(jnp.int32, (32, BLOCK), 0)
    over_first = (((0,), (0,)), ((), ()))
    for b in range(2):
        block = slice(b * BLOCK, (b + 1) * BLOCK)
        shifted = pltpu.roll(ranks_ref[:, block].astype(F32), 30, 0)
        outer = jnp.where((row & 2) == 0, shifted, 0.0).astype(BF16)
        back = lax.dot_general(outer, maps_ref[b * 32:(b + 1) * 32, :], over_first, preferred_element_type=F32)
        back_ref[block, :] = (adapter_scale * back).astype(BF16)


def add_up(in_ref, ids_ref, out_ref, in_f, ids_f):
    in_f[...] = in_ref[...].astype(F32)
    ids_f[...] = ids_ref[...].astype(F32)
    lane = lax.broadcasted_iota(jnp.int32, (PEERS, LANES), 1)
    over_first = (((0,), (0,)), ((), ()))
    total = jnp.zeros((LANES, 8 * LANES), F32)
    for b in range(2):
        which = ids_f[rows_of(4 + b, PEERS, 8), :].astype(jnp.int32)
        chosen = (lane == which).astype(F32).astype(BF16)
        terms = jnp.concatenate(
            [in_f[rows_of(b * 8 + k, PEERS, 16), :] for k in range(8)], axis=1
        ).astype(BF16)
        total += lax.dot_general(chosen, terms, over_first, preferred_element_type=F32)
    for k in range(8):
        out_ref[rows_of(k, 32, 8), :] = total[:32, k * LANES:(k + 1) * LANES]


def unpack(in_ref, down_ref, up_ref, rows_f):
    for m, map_ref in ((0, up_ref), (1, down_ref)):
        for i in range(2):
            rows_f[rows_of(i, PEERS, 2), :] = in_ref[rows_of(2 * m + i, PEERS, 4), :]
        for c in range(BANDS):
            map_ref[:, c * LANES:(c + 1) * LANES] = rows_f[c * 8:(c + 1) * 8, :]


def call(kernel, outs, specs, scratch=(), cost=None, limit=40 * MIB):
    return pl.pallas_call(
        kernel,
        out_shape=[jax.ShapeDtypeStruct(shape, dtype) for shape, dtype in outs],
        in_specs=specs,
        out_specs=[VMEM] * len(outs),
        scratch_shapes=scratch,
        compiler_params=pltpu.CompilerParams(vmem_limit_bytes=limit),
        cost_estimate=cost,
    )


def swap(x):
    chunks = x.reshape(PEERS, x.shape[0] // PEERS, LANES)
    return lax.all_to_all(chunks, "dp", 0, 0, tiled=True).reshape(x.shape)


def from_peer(x, k):
    return lax.ppermute(x, "tensor", [(i, i ^ k) for i in range(4)])


def per_device(attn, output_gradient, down_weight, up_weight, adapter_of_row, lengths):
    width = attn.shape[1]
    me = lax.axis_index("tensor")
    me = me.astype(jnp.int32).reshape(1)
    packed, near, far = call(
        pack_tables,
        [((8 * PEERS, LANES), BF16), ((64, width), BF16), ((128, width), BF16)],
        [SMEM] + [ANY] * 4,
        [
            pltpu.VMEM((8, width), BF16),
            pltpu.VMEM((8, width), BF16),
            pltpu.VMEM((2, BLOCK), jnp.int32),
            pltpu.VMEM((2 * PEERS, LANES), F32),
            pltpu.VMEM((8 * PEERS, LANES), F32),
            pltpu.SemaphoreType.DMA((6,)),
        ],
        limit=56 * MIB,
    )(me, down_weight, up_weight, adapter_of_row.reshape(2, BLOCK), output_gradient)
    live = (adapter_of_row >= 0) & (jnp.arange(2 * BLOCK, dtype=jnp.int32) < lengths[0])
    live = live.astype(F32).reshape(2, BLOCK)
    near, far = from_peer(near, 1), from_peer(far, 2)
    tables = swap(packed)
    tables, near, far = lax.optimization_barrier((tables, near, far))
    pieces = [near, far, from_peer(far[64:], 1)]
    (picked,) = call(
        pick_rows,
        [((16 * PEERS, LANES), BF16)],
        [VMEM],
        [pltpu.VMEM((8 * PEERS, LANES), F32), pltpu.VMEM((16 * PEERS, LANES), F32)],
    )(tables)
    picked = swap(picked)
    maps, grad, part = call(
        project,
        [((64, width), BF16), ((2 * BLOCK, width), BF16), ((32, 2 * BLOCK), F32)],
        [SMEM, VMEM, VMEM, ANY, VMEM, VMEM, VMEM],
        [pltpu.SemaphoreType.DMA(())],
    )(me, picked, attn, output_gradient, *pieces)
    parts = [part] + [from_peer(part, k) for k in (1, 2, 3)]
    ranks, terms = call(
        make_terms,
        [((32, 2 * BLOCK), BF16), ((16 * PEERS, LANES), BF16)],
        [VMEM] * 7,
    )(*parts, live, attn, grad)
    terms = swap(terms)
    (attention_gradient,) = call(
        go_back,
        [((2 * BLOCK, width), BF16)],
        [VMEM] * 2,
        cost=pl.CostEstimate(flops=2 * 32 * 256 * 2048, bytes_accessed=2 << 20, transcendentals=0),
    )(ranks, maps)
    (sums,) = call(
        add_up,
        [((4 * PEERS, LANES), F32)],
        [VMEM, VMEM],
        [pltpu.VMEM((16 * PEERS, LANES), F32), pltpu.VMEM((8 * PEERS, LANES), F32)],
    )(terms, tables)
    sums = swap(sums)
    grad_a, grad_b = call(
        unpack,
        [((8, width), F32), ((8, width), F32)],
        [VMEM],
        [pltpu.VMEM((2 * PEERS, LANES), F32)],
    )(sums)
    return attention_gradient, grad_a, grad_b


def solution(mesh):
    return jax.shard_map(
        per_device,
        mesh=mesh,
        in_specs=(
            P("dp", "tensor"),
            P(("dp", "tensor"), None),
            P("dp", "tensor"),
            P("dp", "tensor"),
            P("dp"),
            P("dp"),
        ),
        out_specs=(P("dp", "tensor"), P("dp", "tensor"), P("dp", "tensor")),
        check_vma=False,
    )
```

```python
import jax
import jax.numpy as jnp
from jax import lax
from jax.experimental import pallas as pl
from jax.experimental.pallas import tpu as pltpu
from jax.sharding import PartitionSpec as P

LANES = 128
BLOCK = 128
PEERS = 64
BANDS = 16
QUARTERS = 4

F32 = jnp.float32
BF16 = jnp.bfloat16

adapter_scale = 2.0

VMEM = pl.BlockSpec(memory_space=pltpu.VMEM)
ANY = pl.BlockSpec(memory_space=pl.ANY)
SMEM = pl.BlockSpec(memory_space=pltpu.SMEM)
MIB = 1024 * 1024


def rows_of(first, size, stride):
    return pl.ds(first, size, stride=stride)


def pack_tables(
    place_ref, down_hbm, up_hbm, label_hbm, grad_hbm,
    out_ref, near_ref, far_ref, down_ref, up_ref, label_ref, rows_f, out_f, sems
):
    width = near_ref.shape[1]
    moves = [(label_hbm, label_ref), (down_hbm, down_ref), (up_hbm, up_ref)]
    for k, piece in ((1, near_ref), (2, far_ref.at[pl.ds(0, 64), :]), (3, far_ref.at[pl.ds(64, 64), :])):
        first = pl.multiple_of(lax.bitwise_xor(place_ref[0], k) * width, width)
        moves.append((grad_hbm.at[:, pl.ds(first, width)], piece))
    copies = [pltpu.make_async_copy(src, dst, sems.at[n]) for n, (src, dst) in enumerate(moves)]
    for copy in copies:
        copy.start()
    for b in range(2):
        out_f[rows_of(6 + b, PEERS, 8), :] = jnp.zeros((PEERS, LANES), F32)
    copies[0].wait()
    labels = label_ref[...]
    for b in range(2):
        which = jnp.maximum(labels[b:b + 1, 0:1], 0).astype(F32)
        out_f[rows_of(4 + b, PEERS, 8), :] = jnp.broadcast_to(which, (PEERS, LANES))
    for m, map_ref in enumerate((down_ref, up_ref)):
        copies[1 + m].wait()
        for c in range(BANDS):
            rows_f[c * 8:(c + 1) * 8, :] = map_ref[:, c * LANES:(c + 1) * LANES].astype(F32)
        for i in range(2):
            out_f[rows_of(2 * m + i, PEERS, 8), :] = rows_f[rows_of(i, PEERS, 2), :]
    out_ref[...] = out_f[...].astype(BF16)
    for copy in copies[3:]:
        copy.wait()


def pick_rows(in_ref, out_ref, in_f, out_f):
    in_f[...] = in_ref[...].astype(F32)
    table = jnp.concatenate([in_f[rows_of(k, PEERS, 8), :] for k in range(4)], axis=1).astype(BF16)
    lane = lax.broadcasted_iota(jnp.int32, (PEERS, LANES), 1)
    for b in range(2):
        which = in_f[rows_of(4 + b, PEERS, 8), :].astype(jnp.int32)
        for h in range(2):
            chosen = (lane == 2 * which + h).astype(F32).astype(BF16)[:, :PEERS]
            picked = jnp.dot(chosen, table, preferred_element_type=F32)
            for k in range(4):
                out_f[rows_of(b * 8 + h * 4 + k, PEERS, 16), :] = picked[:, k * LANES:(k + 1) * LANES]
    out_ref[...] = out_f[...].astype(BF16)


def project(place_ref, picked_ref, attn_ref, tokens_hbm, one_ref, two_ref, three_ref, maps_ref, grad_ref, part_ref, sem):
    me = place_ref[0]
    width = grad_ref.shape[1]
    own = tokens_hbm.at[:, pl.ds(pl.multiple_of(me * width, width), width)]
    copy = pltpu.make_async_copy(own, grad_ref.at[pl.ds(pl.multiple_of(me * 64, 64), 64), :], sem)
    copy.start()
    for k, piece in ((1, one_ref), (2, two_ref), (3, three_ref)):
        first = pl.multiple_of(lax.bitwise_xor(me, k) * 64, 64)
        grad_ref[pl.ds(first, 64), :] = piece[:64, :]
    for c in range(BANDS):
        rows = picked_ref[c * 64:(c + 1) * 64, :].astype(F32).reshape(QUARTERS, 2, 8, LANES)
        for b in range(2):
            maps_ref[b * 32:(b + 1) * 32, c * LANES:(c + 1) * LANES] = rows[:, b].reshape(32, LANES).astype(BF16)
    row = lax.broadcasted_iota(jnp.int32, (32, BLOCK), 0)
    over_last = (((1,), (1,)), ((), ()))
    inners = [
        lax.dot_general(
            maps_ref[b * 32:(b + 1) * 32, :],
            attn_ref[b * BLOCK:(b + 1) * BLOCK, :],
            over_last,
            preferred_element_type=F32,
        )
        for b in range(2)
    ]
    copy.wait()
    for b in range(2):
        maps = maps_ref[b * 32:(b + 1) * 32, :]
        block = slice(b * BLOCK, (b + 1) * BLOCK)
        outer = lax.dot_general(maps, grad_ref[block, :], over_last, preferred_element_type=F32)
        part_ref[:, block] = jnp.where((row & 2) == 0, inners[b], outer)


def make_terms(own_ref, one_ref, two_ref, three_ref, live_ref, attn_ref, grad_ref, ranks_ref, term_ref):
    total = (own_ref[...] + one_ref[...]) + (two_ref[...] + three_ref[...])
    row = lax.broadcasted_iota(jnp.int32, (32, LANES), 0)
    terms = []
    for b in range(2):
        block = slice(b * BLOCK, (b + 1) * BLOCK)
        ranks = jnp.where(live_ref[b:b + 1, :] > 0, total[:, block], 0.0).astype(BF16)
        ranks_ref[:, block] = ranks
        down = jnp.dot(ranks, attn_ref[block, :], preferred_element_type=F32)
        up = jnp.dot(ranks, grad_ref[block, :], preferred_element_type=F32)
        terms.append((down, up))
    for c in range(BANDS):
        band = slice(c * LANES, (c + 1) * LANES)
        both = [
            adapter_scale * jnp.where((row & 2) == 0, up[:, band], down[:, band])
            for down, up in terms
        ]
        for q in range(QUARTERS):
            pair = jnp.concatenate([one[q * 8:(q + 1) * 8] for one in both], axis=0)
            term_ref[c * 64 + q * 16:c * 64 + (q + 1) * 16, :] = pair.astype(BF16)


def go_back(ranks_ref, maps_ref, back_ref):
    row = lax.broadcasted_iota(jnp.int32, (32, BLOCK), 0)
    over_first = (((0,), (0,)), ((), ()))
    for b in range(2):
        block = slice(b * BLOCK, (b + 1) * BLOCK)
        shifted = pltpu.roll(ranks_ref[:, block].astype(F32), 30, 0)
        outer = jnp.where((row & 2) == 0, shifted, 0.0).astype(BF16)
        back = lax.dot_general(outer, maps_ref[b * 32:(b + 1) * 32, :], over_first, preferred_element_type=F32)
        back_ref[block, :] = (adapter_scale * back).astype(BF16)


def add_up(in_ref, ids_ref, out_ref, in_f, ids_f):
    in_f[...] = in_ref[...].astype(F32)
    ids_f[...] = ids_ref[...].astype(F32)
    lane = lax.broadcasted_iota(jnp.int32, (PEERS, LANES), 1)
    over_first = (((0,), (0,)), ((), ()))
    total = jnp.zeros((LANES, 8 * LANES), F32)
    for b in range(2):
        which = ids_f[rows_of(4 + b, PEERS, 8), :].astype(jnp.int32)
        chosen = (lane == which).astype(F32).astype(BF16)
        terms = jnp.concatenate(
            [in_f[rows_of(b * 8 + k, PEERS, 16), :] for k in range(8)], axis=1
        ).astype(BF16)
        total += lax.dot_general(chosen, terms, over_first, preferred_element_type=F32)
    for k in range(8):
        out_ref[rows_of(k, 32, 8), :] = total[:32, k * LANES:(k + 1) * LANES]


def unpack(in_ref, down_ref, up_ref, rows_f):
    for m, map_ref in ((0, up_ref), (1, down_ref)):
        for i in range(2):
            rows_f[rows_of(i, PEERS, 2), :] = in_ref[rows_of(2 * m + i, PEERS, 4), :]
        for c in range(BANDS):
            map_ref[:, c * LANES:(c + 1) * LANES] = rows_f[c * 8:(c + 1) * 8, :]


def call(kernel, outs, specs, scratch=(), cost=None, limit=40 * MIB, places=None):
    return pl.pallas_call(
        kernel,
        out_shape=[jax.ShapeDtypeStruct(shape, dtype) for shape, dtype in outs],
        in_specs=specs,
        out_specs=places or [VMEM] * len(outs),
        scratch_shapes=scratch,
        compiler_params=pltpu.CompilerParams(vmem_limit_bytes=limit),
        cost_estimate=cost,
    )


def swap(x):
    chunks = x.reshape(PEERS, x.shape[0] // PEERS, LANES)
    return lax.all_to_all(chunks, "dp", 0, 0, tiled=True).reshape(x.shape)


def from_peer(x, k):
    return lax.ppermute(x, "tensor", [(i, i ^ k) for i in range(4)])


def per_device(attn, output_gradient, down_weight, up_weight, adapter_of_row, lengths):
    width = attn.shape[1]
    me = lax.axis_index("tensor")
    me = me.astype(jnp.int32).reshape(1)
    packed, near, far = call(
        pack_tables,
        [((8 * PEERS, LANES), BF16), ((64, width), BF16), ((128, width), BF16)],
        [SMEM] + [ANY] * 4,
        [
            pltpu.VMEM((8, width), BF16),
            pltpu.VMEM((8, width), BF16),
            pltpu.VMEM((2, BLOCK), jnp.int32),
            pltpu.VMEM((2 * PEERS, LANES), F32),
            pltpu.VMEM((8 * PEERS, LANES), F32),
            pltpu.SemaphoreType.DMA((6,)),
        ],
        limit=56 * MIB,
        places=[VMEM, ANY, ANY],
    )(me, down_weight, up_weight, adapter_of_row.reshape(2, BLOCK), output_gradient)
    live = (adapter_of_row >= 0) & (jnp.arange(2 * BLOCK, dtype=jnp.int32) < lengths[0])
    live = live.astype(F32).reshape(2, BLOCK)
    near, far = from_peer(near, 1), from_peer(far, 2)
    tables = swap(packed)
    tables, near, far = lax.optimization_barrier((tables, near, far))
    odd, live = lax.optimization_barrier((from_peer(far[64:], 1), live))
    pieces = [near, far, odd]
    (picked,) = call(
        pick_rows,
        [((16 * PEERS, LANES), BF16)],
        [VMEM],
        [pltpu.VMEM((8 * PEERS, LANES), F32), pltpu.VMEM((16 * PEERS, LANES), F32)],
    )(tables)
    picked = swap(picked)
    maps, grad, part = call(
        project,
        [((64, width), BF16), ((2 * BLOCK, width), BF16), ((32, 2 * BLOCK), F32)],
        [SMEM, VMEM, VMEM, ANY, VMEM, VMEM, VMEM],
        [pltpu.SemaphoreType.DMA(())],
    )(me, picked, attn, output_gradient, *pieces)
    parts = [part] + [from_peer(part, k) for k in (1, 2, 3)]
    ranks, terms = call(
        make_terms,
        [((32, 2 * BLOCK), BF16), ((16 * PEERS, LANES), BF16)],
        [VMEM] * 7,
    )(*parts, live, attn, grad)
    terms = swap(terms)
    (attention_gradient,) = call(
        go_back,
        [((2 * BLOCK, width), BF16)],
        [VMEM] * 2,
        cost=pl.CostEstimate(flops=2 * 32 * 256 * 2048, bytes_accessed=2 << 20, transcendentals=0),
    )(ranks, maps)
    (sums,) = call(
        add_up,
        [((4 * PEERS, LANES), F32)],
        [VMEM, VMEM],
        [pltpu.VMEM((16 * PEERS, LANES), F32), pltpu.VMEM((8 * PEERS, LANES), F32)],
    )(terms, tables)
    sums = swap(sums)
    grad_a, grad_b = call(
        unpack,
        [((8, width), F32), ((8, width), F32)],
        [VMEM],
        [pltpu.VMEM((2 * PEERS, LANES), F32)],
    )(sums)
    return attention_gradient, grad_a, grad_b


def solution(mesh):
    return jax.shard_map(
        per_device,
        mesh=mesh,
        in_specs=(
            P("dp", "tensor"),
            P(("dp", "tensor"), None),
            P("dp", "tensor"),
            P("dp", "tensor"),
            P("dp"),
            P("dp"),
        ),
        out_specs=(P("dp", "tensor"), P("dp", "tensor"), P("dp", "tensor")),
        check_vma=False,
    )
```

```python
import jax
import jax.numpy as jnp
from jax import lax
from jax.experimental import pallas as pl
from jax.experimental.pallas import tpu as pltpu
from jax.sharding import PartitionSpec as P

LANES = 128
BLOCK = 128
PEERS = 64
BANDS = 16
QUARTERS = 4

F32 = jnp.float32
BF16 = jnp.bfloat16

adapter_scale = 2.0

VMEM = pl.BlockSpec(memory_space=pltpu.VMEM)
ANY = pl.BlockSpec(memory_space=pl.ANY)
SMEM = pl.BlockSpec(memory_space=pltpu.SMEM)
MIB = 1024 * 1024


def rows_of(first, size, stride):
    return pl.ds(first, size, stride=stride)


def pack_tables(
    place_ref, down_hbm, up_hbm, label_hbm, grad_hbm,
    out_ref, near_hbm, far_hbm, down_ref, up_ref, label_ref, rows_f, out_f, cut_ref, sems
):
    width = down_ref.shape[1]
    moves = [(label_hbm, label_ref), (down_hbm, down_ref), (up_hbm, up_ref)]
    slots = [cut_ref.at[pl.ds(n * 64, 64), :] for n in range(3)]
    for n in range(3):
        first = pl.multiple_of(lax.bitwise_xor(place_ref[0], (2, 3, 1)[n]) * width, width)
        moves.append((grad_hbm.at[:, pl.ds(first, width)], slots[n]))
    ends = (far_hbm.at[pl.ds(0, 64), :], far_hbm.at[pl.ds(64, 64), :], near_hbm)
    copies = [pltpu.make_async_copy(src, dst, sems.at[n]) for n, (src, dst) in enumerate(moves)]
    for copy in copies:
        copy.start()
    for b in range(2):
        out_f[rows_of(6 + b, PEERS, 8), :] = jnp.zeros((PEERS, LANES), F32)
    copies[0].wait()
    labels = label_ref[...]
    for b in range(2):
        which = jnp.maximum(labels[b:b + 1, 0:1], 0).astype(F32)
        out_f[rows_of(4 + b, PEERS, 8), :] = jnp.broadcast_to(which, (PEERS, LANES))
    for m, map_ref in enumerate((down_ref, up_ref)):
        copies[1 + m].wait()
        for c in range(BANDS):
            rows_f[c * 8:(c + 1) * 8, :] = map_ref[:, c * LANES:(c + 1) * LANES].astype(F32)
        for i in range(2):
            out_f[rows_of(2 * m + i, PEERS, 8), :] = rows_f[rows_of(i, PEERS, 2), :]
    backs = [pltpu.make_async_copy(slots[n], ends[n], sems.at[6 + n]) for n in range(3)]
    for copy, back in zip(copies[3:], backs):
        copy.wait()
        back.start()
    out_ref[...] = out_f[...].astype(BF16)
    for back in backs:
        back.wait()


def pick_rows(in_ref, out_ref, in_f, out_f):
    in_f[...] = in_ref[...].astype(F32)
    table = jnp.concatenate([in_f[rows_of(k, PEERS, 8), :] for k in range(4)], axis=1).astype(BF16)
    lane = lax.broadcasted_iota(jnp.int32, (PEERS, LANES), 1)
    for b in range(2):
        which = in_f[rows_of(4 + b, PEERS, 8), :].astype(jnp.int32)
        for h in range(2):
            chosen = (lane == 2 * which + h).astype(F32).astype(BF16)[:, :PEERS]
            picked = jnp.dot(chosen, table, preferred_element_type=F32)
            for k in range(4):
                out_f[rows_of(b * 8 + h * 4 + k, PEERS, 16), :] = picked[:, k * LANES:(k + 1) * LANES]
    out_ref[...] = out_f[...].astype(BF16)


def project(place_ref, picked_ref, attn_ref, tokens_ref, one_ref, two_ref, three_ref, maps_ref, grad_ref, part_ref):
    me = place_ref[0]
    width = grad_ref.shape[1]
    own = tokens_ref[:, pl.ds(pl.multiple_of(me * width, width), width)]
    grad_ref[pl.ds(pl.multiple_of(me * 64, 64), 64), :] = own
    for k, piece in ((1, one_ref), (2, two_ref), (3, three_ref)):
        first = pl.multiple_of(lax.bitwise_xor(me, k) * 64, 64)
        grad_ref[pl.ds(first, 64), :] = piece[:64, :]
    for c in range(BANDS):
        rows = picked_ref[c * 64:(c + 1) * 64, :].astype(F32).reshape(QUARTERS, 2, 8, LANES)
        for b in range(2):
            maps_ref[b * 32:(b + 1) * 32, c * LANES:(c + 1) * LANES] = rows[:, b].reshape(32, LANES).astype(BF16)
    row = lax.broadcasted_iota(jnp.int32, (32, BLOCK), 0)
    over_last = (((1,), (1,)), ((), ()))
    for b in range(2):
        maps = maps_ref[b * 32:(b + 1) * 32, :]
        block = slice(b * BLOCK, (b + 1) * BLOCK)
        inner = lax.dot_general(maps, attn_ref[block, :], over_last, preferred_element_type=F32)
        outer = lax.dot_general(maps, grad_ref[block, :], over_last, preferred_element_type=F32)
        part_ref[:, block] = jnp.where((row & 2) == 0, inner, outer)


def make_terms(own_ref, one_ref, two_ref, three_ref, live_ref, attn_ref, grad_ref, ranks_ref, term_ref):
    total = (own_ref[...] + one_ref[...]) + (two_ref[...] + three_ref[...])
    row = lax.broadcasted_iota(jnp.int32, (32, LANES), 0)
    terms = []
    for b in range(2):
        block = slice(b * BLOCK, (b + 1) * BLOCK)
        ranks = jnp.where(live_ref[b:b + 1, :] > 0, total[:, block], 0.0).astype(BF16)
        ranks_ref[:, block] = ranks
        down = jnp.dot(ranks, attn_ref[block, :], preferred_element_type=F32)
        up = jnp.dot(ranks, grad_ref[block, :], preferred_element_type=F32)
        terms.append((down, up))
    for c in range(BANDS):
        band = slice(c * LANES, (c + 1) * LANES)
        both = [
            adapter_scale * jnp.where((row & 2) == 0, up[:, band], down[:, band])
            for down, up in terms
        ]
        for q in range(QUARTERS):
            pair = jnp.concatenate([one[q * 8:(q + 1) * 8] for one in both], axis=0)
            term_ref[c * 64 + q * 16:c * 64 + (q + 1) * 16, :] = pair.astype(BF16)


def go_back(ranks_ref, maps_ref, back_ref):
    row = lax.broadcasted_iota(jnp.int32, (32, BLOCK), 0)
    over_first = (((0,), (0,)), ((), ()))
    for b in range(2):
        block = slice(b * BLOCK, (b + 1) * BLOCK)
        shifted = pltpu.roll(ranks_ref[:, block].astype(F32), 30, 0)
        outer = jnp.where((row & 2) == 0, shifted, 0.0).astype(BF16)
        back = lax.dot_general(outer, maps_ref[b * 32:(b + 1) * 32, :], over_first, preferred_element_type=F32)
        back_ref[block, :] = (adapter_scale * back).astype(BF16)


def add_up(in_ref, ids_ref, out_ref, in_f, ids_f):
    in_f[...] = in_ref[...].astype(F32)
    ids_f[...] = ids_ref[...].astype(F32)
    lane = lax.broadcasted_iota(jnp.int32, (PEERS, LANES), 1)
    over_first = (((0,), (0,)), ((), ()))
    total = jnp.zeros((LANES, 8 * LANES), F32)
    for b in range(2):
        which = ids_f[rows_of(4 + b, PEERS, 8), :].astype(jnp.int32)
        chosen = (lane == which).astype(F32).astype(BF16)
        terms = jnp.concatenate(
            [in_f[rows_of(b * 8 + k, PEERS, 16), :] for k in range(8)], axis=1
        ).astype(BF16)
        total += lax.dot_general(chosen, terms, over_first, preferred_element_type=F32)
    for k in range(8):
        out_ref[rows_of(k, 32, 8), :] = total[:32, k * LANES:(k + 1) * LANES]


def unpack(in_ref, down_ref, up_ref, rows_f):
    for m, map_ref in ((0, up_ref), (1, down_ref)):
        for i in range(2):
            rows_f[rows_of(i, PEERS, 2), :] = in_ref[rows_of(2 * m + i, PEERS, 4), :]
        for c in range(BANDS):
            map_ref[:, c * LANES:(c + 1) * LANES] = rows_f[c * 8:(c + 1) * 8, :]


def call(kernel, outs, specs, scratch=(), cost=None, limit=40 * MIB, places=None):
    return pl.pallas_call(
        kernel,
        out_shape=[jax.ShapeDtypeStruct(shape, dtype) for shape, dtype in outs],
        in_specs=specs,
        out_specs=places or [VMEM] * len(outs),
        scratch_shapes=scratch,
        compiler_params=pltpu.CompilerParams(vmem_limit_bytes=limit),
        cost_estimate=cost,
    )


def swap(x):
    chunks = x.reshape(PEERS, x.shape[0] // PEERS, LANES)
    return lax.all_to_all(chunks, "dp", 0, 0, tiled=True).reshape(x.shape)


def from_peer(x, k):
    return lax.ppermute(x, "tensor", [(i, i ^ k) for i in range(4)])


def per_device(attn, output_gradient, down_weight, up_weight, adapter_of_row, lengths):
    width = attn.shape[1]
    me = lax.axis_index("tensor")
    me = me.astype(jnp.int32).reshape(1)
    packed, near, far = call(
        pack_tables,
        [((8 * PEERS, LANES), BF16), ((64, width), BF16), ((128, width), BF16)],
        [SMEM] + [ANY] * 4,
        [
            pltpu.VMEM((8, width), BF16),
            pltpu.VMEM((8, width), BF16),
            pltpu.VMEM((2, BLOCK), jnp.int32),
            pltpu.VMEM((2 * PEERS, LANES), F32),
            pltpu.VMEM((8 * PEERS, LANES), F32),
            pltpu.VMEM((192, width), BF16),
            pltpu.SemaphoreType.DMA((9,)),
        ],
        limit=56 * MIB,
        places=[VMEM, ANY, ANY],
    )(me, down_weight, up_weight, adapter_of_row.reshape(2, BLOCK), output_gradient)
    live = (adapter_of_row >= 0) & (jnp.arange(2 * BLOCK, dtype=jnp.int32) < lengths[0])
    live = live.astype(F32).reshape(2, BLOCK)
    near, far = from_peer(near, 1), from_peer(far, 2)
    tables = swap(packed)
    tables, near, far = lax.optimization_barrier((tables, near, far))
    odd, live = lax.optimization_barrier((from_peer(far[64:], 1), live))
    pieces = [near, far, odd]
    (picked,) = call(
        pick_rows,
        [((16 * PEERS, LANES), BF16)],
        [VMEM],
        [pltpu.VMEM((8 * PEERS, LANES), F32), pltpu.VMEM((16 * PEERS, LANES), F32)],
    )(tables)
    picked = swap(picked)
    maps, grad, part = call(
        project,
        [((64, width), BF16), ((2 * BLOCK, width), BF16), ((32, 2 * BLOCK), F32)],
        [SMEM] + [VMEM] * 6,
    )(me, picked, attn, output_gradient, *pieces)
    parts = [part] + [from_peer(part, k) for k in (1, 2, 3)]
    ranks, terms = call(
        make_terms,
        [((32, 2 * BLOCK), BF16), ((16 * PEERS, LANES), BF16)],
        [VMEM] * 7,
    )(*parts, live, attn, grad)
    terms = swap(terms)
    (attention_gradient,) = call(
        go_back,
        [((2 * BLOCK, width), BF16)],
        [VMEM] * 2,
        cost=pl.CostEstimate(flops=2 * 32 * 256 * 2048, bytes_accessed=2 << 20, transcendentals=0),
    )(ranks, maps)
    terms, attention_gradient = lax.optimization_barrier((terms, attention_gradient))
    (sums,) = call(
        add_up,
        [((4 * PEERS, LANES), F32)],
        [VMEM, VMEM],
        [pltpu.VMEM((16 * PEERS, LANES), F32), pltpu.VMEM((8 * PEERS, LANES), F32)],
    )(terms, tables)
    sums = swap(sums)
    grad_a, grad_b = call(
        unpack,
        [((8, width), F32), ((8, width), F32)],
        [VMEM],
        [pltpu.VMEM((2 * PEERS, LANES), F32)],
    )(sums)
    return attention_gradient, grad_a, grad_b


def solution(mesh):
    return jax.shard_map(
        per_device,
        mesh=mesh,
        in_specs=(
            P("dp", "tensor"),
            P(("dp", "tensor"), None),
            P("dp", "tensor"),
            P("dp", "tensor"),
            P("dp"),
            P("dp"),
        ),
        out_specs=(P("dp", "tensor"), P("dp", "tensor"), P("dp", "tensor")),
        check_vma=False,
    )
```

```python
import jax
import jax.numpy as jnp
from jax import lax
from jax.experimental import pallas as pl
from jax.experimental.pallas import tpu as pltpu
from jax.sharding import PartitionSpec as P

LANES = 128
BLOCK = 128
PEERS = 64
BANDS = 16
QUARTERS = 4

F32 = jnp.float32
BF16 = jnp.bfloat16

adapter_scale = 2.0

VMEM = pl.BlockSpec(memory_space=pltpu.VMEM)
ANY = pl.BlockSpec(memory_space=pl.ANY)
SMEM = pl.BlockSpec(memory_space=pltpu.SMEM)
MIB = 1024 * 1024


def rows_of(first, size, stride):
    return pl.ds(first, size, stride=stride)


def pack_tables(down_hbm, up_hbm, label_hbm, out_ref, down_ref, up_ref, label_ref, rows_f, out_f, sems):
    moves = ((label_hbm, label_ref), (down_hbm, down_ref), (up_hbm, up_ref))
    copies = [pltpu.make_async_copy(src, dst, sems.at[n]) for n, (src, dst) in enumerate(moves)]
    for copy in copies:
        copy.start()
    for b in range(2):
        out_f[rows_of(6 + b, PEERS, 8), :] = jnp.zeros((PEERS, LANES), F32)
    copies[0].wait()
    labels = label_ref[...]
    for b in range(2):
        which = jnp.maximum(labels[b:b + 1, 0:1], 0).astype(F32)
        out_f[rows_of(4 + b, PEERS, 8), :] = jnp.broadcast_to(which, (PEERS, LANES))
    for m, map_ref in enumerate((down_ref, up_ref)):
        copies[1 + m].wait()
        for c in range(BANDS):
            rows_f[c * 8:(c + 1) * 8, :] = map_ref[:, c * LANES:(c + 1) * LANES].astype(F32)
        for i in range(2):
            out_f[rows_of(2 * m + i, PEERS, 8), :] = rows_f[rows_of(i, PEERS, 2), :]
    out_ref[...] = out_f[...].astype(BF16)


def cut_tokens(place_ref, grad_hbm, packed_hbm, near_ref, far_ref, sems):
    width = near_ref.shape[1]
    copies = []
    for k, piece in ((2, far_ref.at[pl.ds(0, 64), :]), (3, far_ref.at[pl.ds(64, 64), :]), (1, near_ref)):
        first = pl.multiple_of(lax.bitwise_xor(place_ref[0], k) * width, width)
        copies.append(pltpu.make_async_copy(grad_hbm.at[:, pl.ds(first, width)], piece, sems.at[k - 1]))
    for copy in copies:
        copy.start()
    for copy in copies:
        copy.wait()


def pick_rows(in_ref, out_ref, in_f, out_f):
    in_f[...] = in_ref[...].astype(F32)
    table = jnp.concatenate([in_f[rows_of(k, PEERS, 8), :] for k in range(4)], axis=1).astype(BF16)
    lane = lax.broadcasted_iota(jnp.int32, (PEERS, LANES), 1)
    for b in range(2):
        which = in_f[rows_of(4 + b, PEERS, 8), :].astype(jnp.int32)
        for h in range(2):
            chosen = (lane == 2 * which + h).astype(F32).astype(BF16)[:, :PEERS]
            picked = jnp.dot(chosen, table, preferred_element_type=F32)
            for k in range(4):
                out_f[rows_of(b * 8 + h * 4 + k, PEERS, 16), :] = picked[:, k * LANES:(k + 1) * LANES]
    out_ref[...] = out_f[...].astype(BF16)


def project(place_ref, picked_ref, attn_ref, tokens_ref, one_ref, two_ref, three_ref, maps_ref, grad_ref, part_ref):
    me = place_ref[0]
    width = grad_ref.shape[1]
    own = tokens_ref[:, pl.ds(pl.multiple_of(me * width, width), width)]
    grad_ref[pl.ds(pl.multiple_of(me * 64, 64), 64), :] = own
    for k, piece in ((1, one_ref), (2, two_ref), (3, three_ref)):
        first = pl.multiple_of(lax.bitwise_xor(me, k) * 64, 64)
        grad_ref[pl.ds(first, 64), :] = piece[:64, :]
    for c in range(BANDS):
        rows = picked_ref[c * 64:(c + 1) * 64, :].astype(F32).reshape(QUARTERS, 2, 8, LANES)
        for b in range(2):
            maps_ref[b * 32:(b + 1) * 32, c * LANES:(c + 1) * LANES] = rows[:, b].reshape(32, LANES).astype(BF16)
    row = lax.broadcasted_iota(jnp.int32, (32, BLOCK), 0)
    over_last = (((1,), (1,)), ((), ()))
    for b in range(2):
        maps = maps_ref[b * 32:(b + 1) * 32, :]
        block = slice(b * BLOCK, (b + 1) * BLOCK)
        inner = lax.dot_general(maps, attn_ref[block, :], over_last, preferred_element_type=F32)
        outer = lax.dot_general(maps, grad_ref[block, :], over_last, preferred_element_type=F32)
        part_ref[:, block] = jnp.where((row & 2) == 0, inner, outer)


def make_terms(own_ref, one_ref, two_ref, three_ref, live_ref, attn_ref, grad_ref, ranks_ref, term_ref):
    total = (own_ref[...] + one_ref[...]) + (two_ref[...] + three_ref[...])
    row = lax.broadcasted_iota(jnp.int32, (32, LANES), 0)
    terms = []
    for b in range(2):
        block = slice(b * BLOCK, (b + 1) * BLOCK)
        ranks = jnp.where(live_ref[b:b + 1, :] > 0, total[:, block], 0.0).astype(BF16)
        ranks_ref[:, block] = ranks
        down = jnp.dot(ranks, attn_ref[block, :], preferred_element_type=F32)
        up = jnp.dot(ranks, grad_ref[block, :], preferred_element_type=F32)
        terms.append((down, up))
    for c in range(BANDS):
        band = slice(c * LANES, (c + 1) * LANES)
        both = [
            adapter_scale * jnp.where((row & 2) == 0, up[:, band], down[:, band])
            for down, up in terms
        ]
        for q in range(QUARTERS):
            pair = jnp.concatenate([one[q * 8:(q + 1) * 8] for one in both], axis=0)
            term_ref[c * 64 + q * 16:c * 64 + (q + 1) * 16, :] = pair.astype(BF16)


def go_back(ranks_ref, maps_ref, back_ref):
    row = lax.broadcasted_iota(jnp.int32, (32, BLOCK), 0)
    over_first = (((0,), (0,)), ((), ()))
    for b in range(2):
        block = slice(b * BLOCK, (b + 1) * BLOCK)
        shifted = pltpu.roll(ranks_ref[:, block].astype(F32), 30, 0)
        outer = jnp.where((row & 2) == 0, shifted, 0.0).astype(BF16)
        back = lax.dot_general(outer, maps_ref[b * 32:(b + 1) * 32, :], over_first, preferred_element_type=F32)
        back_ref[block, :] = (adapter_scale * back).astype(BF16)


def add_up(in_ref, ids_ref, out_ref, in_f, ids_f):
    in_f[...] = in_ref[...].astype(F32)
    ids_f[...] = ids_ref[...].astype(F32)
    lane = lax.broadcasted_iota(jnp.int32, (PEERS, LANES), 1)
    over_first = (((0,), (0,)), ((), ()))
    total = jnp.zeros((LANES, 8 * LANES), F32)
    for b in range(2):
        which = ids_f[rows_of(4 + b, PEERS, 8), :].astype(jnp.int32)
        chosen = (lane == which).astype(F32).astype(BF16)
        terms = jnp.concatenate(
            [in_f[rows_of(b * 8 + k, PEERS, 16), :] for k in range(8)], axis=1
        ).astype(BF16)
        total += lax.dot_general(chosen, terms, over_first, preferred_element_type=F32)
    for k in range(8):
        out_ref[rows_of(k, 32, 8), :] = total[:32, k * LANES:(k + 1) * LANES]


def unpack(in_ref, down_ref, up_ref, rows_f):
    for m, map_ref in ((0, up_ref), (1, down_ref)):
        for i in range(2):
            rows_f[rows_of(i, PEERS, 2), :] = in_ref[rows_of(2 * m + i, PEERS, 4), :]
        for c in range(BANDS):
            map_ref[:, c * LANES:(c + 1) * LANES] = rows_f[c * 8:(c + 1) * 8, :]


def call(kernel, outs, specs, scratch=(), cost=None, limit=40 * MIB):
    return pl.pallas_call(
        kernel,
        out_shape=[jax.ShapeDtypeStruct(shape, dtype) for shape, dtype in outs],
        in_specs=specs,
        out_specs=[VMEM] * len(outs),
        scratch_shapes=scratch,
        compiler_params=pltpu.CompilerParams(vmem_limit_bytes=limit),
        cost_estimate=cost,
    )


def swap(x):
    chunks = x.reshape(PEERS, x.shape[0] // PEERS, LANES)
    return lax.all_to_all(chunks, "dp", 0, 0, tiled=True).reshape(x.shape)


def from_peer(x, k):
    return lax.ppermute(x, "tensor", [(i, i ^ k) for i in range(4)])


def per_device(attn, output_gradient, down_weight, up_weight, adapter_of_row, lengths):
    width = attn.shape[1]
    me = lax.axis_index("tensor")
    me = me.astype(jnp.int32).reshape(1)
    (packed,) = call(
        pack_tables,
        [((8 * PEERS, LANES), BF16)],
        [ANY] * 3,
        [
            pltpu.VMEM((8, width), BF16),
            pltpu.VMEM((8, width), BF16),
            pltpu.VMEM((2, BLOCK), jnp.int32),
            pltpu.VMEM((2 * PEERS, LANES), F32),
            pltpu.VMEM((8 * PEERS, LANES), F32),
            pltpu.SemaphoreType.DMA((3,)),
        ],
        limit=56 * MIB,
    )(down_weight, up_weight, adapter_of_row.reshape(2, BLOCK))
    near, far = call(
        cut_tokens,
        [((64, width), BF16), ((128, width), BF16)],
        [SMEM, ANY, ANY],
        [pltpu.SemaphoreType.DMA((3,))],
        limit=56 * MIB,
    )(me, output_gradient, packed)
    live = (adapter_of_row >= 0) & (jnp.arange(2 * BLOCK, dtype=jnp.int32) < lengths[0])
    live = live.astype(F32).reshape(2, BLOCK)
    tables = swap(packed)
    tables, near, far = lax.optimization_barrier((tables, near, far))
    near, far = from_peer(near, 1), from_peer(far, 2)
    odd, live = lax.optimization_barrier((from_peer(far[64:], 1), live))
    pieces = [near, far, odd]
    (picked,) = call(
        pick_rows,
        [((16 * PEERS, LANES), BF16)],
        [VMEM],
        [pltpu.VMEM((8 * PEERS, LANES), F32), pltpu.VMEM((16 * PEERS, LANES), F32)],
    )(tables)
    picked = swap(picked)
    maps, grad, part = call(
        project,
        [((64, width), BF16), ((2 * BLOCK, width), BF16), ((32, 2 * BLOCK), F32)],
        [SMEM] + [VMEM] * 6,
    )(me, picked, attn, output_gradient, *pieces)
    parts = [part] + [from_peer(part, k) for k in (1, 2, 3)]
    ranks, terms = call(
        make_terms,
        [((32, 2 * BLOCK), BF16), ((16 * PEERS, LANES), BF16)],
        [VMEM] * 7,
    )(*parts, live, attn, grad)
    terms = swap(terms)
    (attention_gradient,) = call(
        go_back,
        [((2 * BLOCK, width), BF16)],
        [VMEM] * 2,
        cost=pl.CostEstimate(flops=2 * 32 * 256 * 2048, bytes_accessed=2 << 20, transcendentals=0),
    )(ranks, maps)
    (sums,) = call(
        add_up,
        [((4 * PEERS, LANES), F32)],
        [VMEM, VMEM],
        [pltpu.VMEM((16 * PEERS, LANES), F32), pltpu.VMEM((8 * PEERS, LANES), F32)],
    )(terms, tables)
    sums = swap(sums)
    grad_a, grad_b = call(
        unpack,
        [((8, width), F32), ((8, width), F32)],
        [VMEM],
        [pltpu.VMEM((2 * PEERS, LANES), F32)],
    )(sums)
    return attention_gradient, grad_a, grad_b


def solution(mesh):
    return jax.shard_map(
        per_device,
        mesh=mesh,
        in_specs=(
            P("dp", "tensor"),
            P(("dp", "tensor"), None),
            P("dp", "tensor"),
            P("dp", "tensor"),
            P("dp"),
            P("dp"),
        ),
        out_specs=(P("dp", "tensor"), P("dp", "tensor"), P("dp", "tensor")),
        check_vma=False,
    )
```

```python
import functools

import jax
import jax.numpy as jnp
from jax import lax
from jax.experimental import pallas as pl
from jax.experimental.pallas import tpu as pltpu
from jax.sharding import PartitionSpec as P

LANES = 128
BLOCK = 128
PEERS = 64
BANDS = 16
QUARTERS = 4

F32 = jnp.float32
BF16 = jnp.bfloat16

adapter_scale = 2.0

VMEM = pl.BlockSpec(memory_space=pltpu.VMEM)
ANY = pl.BlockSpec(memory_space=pl.ANY)
SMEM = pl.BlockSpec(memory_space=pltpu.SMEM)
MIB = 1024 * 1024


def rows_of(first, size, stride):
    return pl.ds(first, size, stride=stride)


def pack_tables(down_hbm, up_hbm, label_hbm, out_ref, down_ref, up_ref, label_ref, rows_f, out_f, sems):
    moves = ((label_hbm, label_ref), (down_hbm, down_ref), (up_hbm, up_ref))
    copies = [pltpu.make_async_copy(src, dst, sems.at[n]) for n, (src, dst) in enumerate(moves)]
    for copy in copies:
        copy.start()
    for b in range(2):
        out_f[rows_of(6 + b, PEERS, 8), :] = jnp.zeros((PEERS, LANES), F32)
    copies[0].wait()
    labels = label_ref[...]
    for b in range(2):
        which = jnp.maximum(labels[b:b + 1, 0:1], 0).astype(F32)
        out_f[rows_of(4 + b, PEERS, 8), :] = jnp.broadcast_to(which, (PEERS, LANES))
    for m, map_ref in enumerate((down_ref, up_ref)):
        copies[1 + m].wait()
        for c in range(BANDS):
            rows_f[c * 8:(c + 1) * 8, :] = map_ref[:, c * LANES:(c + 1) * LANES].astype(F32)
        for i in range(2):
            out_f[rows_of(2 * m + i, PEERS, 8), :] = rows_f[rows_of(i, PEERS, 2), :]
    out_ref[...] = out_f[...].astype(BF16)


def cut_tokens(ks, place_ref, grad_hbm, packed_hbm, out_ref, sems):
    width = out_ref.shape[1]
    copies = []
    for n, k in enumerate(ks):
        first = pl.multiple_of(lax.bitwise_xor(place_ref[0], k) * width, width)
        piece = out_ref.at[pl.ds(n * 64, 64), :]
        copies.append(pltpu.make_async_copy(grad_hbm.at[:, pl.ds(first, width)], piece, sems.at[n]))
    for copy in copies:
        copy.start()
    for copy in copies:
        copy.wait()


def pick_rows(in_ref, out_ref, in_f, out_f):
    in_f[...] = in_ref[...].astype(F32)
    table = jnp.concatenate([in_f[rows_of(k, PEERS, 8), :] for k in range(4)], axis=1).astype(BF16)
    lane = lax.broadcasted_iota(jnp.int32, (PEERS, LANES), 1)
    for b in range(2):
        which = in_f[rows_of(4 + b, PEERS, 8), :].astype(jnp.int32)
        for h in range(2):
            chosen = (lane == 2 * which + h).astype(F32).astype(BF16)[:, :PEERS]
            picked = jnp.dot(chosen, table, preferred_element_type=F32)
            for k in range(4):
                out_f[rows_of(b * 8 + h * 4 + k, PEERS, 16), :] = picked[:, k * LANES:(k + 1) * LANES]
    out_ref[...] = out_f[...].astype(BF16)


def project(place_ref, picked_ref, attn_ref, tokens_ref, one_ref, two_ref, three_ref, maps_ref, grad_ref, part_ref):
    me = place_ref[0]
    width = grad_ref.shape[1]
    own = tokens_ref[:, pl.ds(pl.multiple_of(me * width, width), width)]
    grad_ref[pl.ds(pl.multiple_of(me * 64, 64), 64), :] = own
    for k, piece in ((1, one_ref), (2, two_ref), (3, three_ref)):
        first = pl.multiple_of(lax.bitwise_xor(me, k) * 64, 64)
        grad_ref[pl.ds(first, 64), :] = piece[:64, :]
    for c in range(BANDS):
        rows = picked_ref[c * 64:(c + 1) * 64, :].astype(F32).reshape(QUARTERS, 2, 8, LANES)
        for b in range(2):
            maps_ref[b * 32:(b + 1) * 32, c * LANES:(c + 1) * LANES] = rows[:, b].reshape(32, LANES).astype(BF16)
    row = lax.broadcasted_iota(jnp.int32, (32, BLOCK), 0)
    over_last = (((1,), (1,)), ((), ()))
    for b in range(2):
        maps = maps_ref[b * 32:(b + 1) * 32, :]
        block = slice(b * BLOCK, (b + 1) * BLOCK)
        inner = lax.dot_general(maps, attn_ref[block, :], over_last, preferred_element_type=F32)
        outer = lax.dot_general(maps, grad_ref[block, :], over_last, preferred_element_type=F32)
        part_ref[:, block] = jnp.where((row & 2) == 0, inner, outer)


def make_terms(own_ref, one_ref, two_ref, three_ref, live_ref, attn_ref, grad_ref, ranks_ref, term_ref):
    total = (own_ref[...] + one_ref[...]) + (two_ref[...] + three_ref[...])
    row = lax.broadcasted_iota(jnp.int32, (32, LANES), 0)
    terms = []
    for b in range(2):
        block = slice(b * BLOCK, (b + 1) * BLOCK)
        ranks = jnp.where(live_ref[b:b + 1, :] > 0, total[:, block], 0.0).astype(BF16)
        ranks_ref[:, block] = ranks
        down = jnp.dot(ranks, attn_ref[block, :], preferred_element_type=F32)
        up = jnp.dot(ranks, grad_ref[block, :], preferred_element_type=F32)
        terms.append((down, up))
    for c in range(BANDS):
        band = slice(c * LANES, (c + 1) * LANES)
        both = [
            adapter_scale * jnp.where((row & 2) == 0, up[:, band], down[:, band])
            for down, up in terms
        ]
        for q in range(QUARTERS):
            pair = jnp.concatenate([one[q * 8:(q + 1) * 8] for one in both], axis=0)
            term_ref[c * 64 + q * 16:c * 64 + (q + 1) * 16, :] = pair.astype(BF16)


def go_back(ranks_ref, maps_ref, back_ref):
    row = lax.broadcasted_iota(jnp.int32, (32, BLOCK), 0)
    over_first = (((0,), (0,)), ((), ()))
    for b in range(2):
        block = slice(b * BLOCK, (b + 1) * BLOCK)
        shifted = pltpu.roll(ranks_ref[:, block].astype(F32), 30, 0)
        outer = jnp.where((row & 2) == 0, shifted, 0.0).astype(BF16)
        back = lax.dot_general(outer, maps_ref[b * 32:(b + 1) * 32, :], over_first, preferred_element_type=F32)
        back_ref[block, :] = (adapter_scale * back).astype(BF16)


def add_up(in_ref, ids_ref, out_ref, in_f, ids_f):
    in_f[...] = in_ref[...].astype(F32)
    ids_f[...] = ids_ref[...].astype(F32)
    lane = lax.broadcasted_iota(jnp.int32, (PEERS, LANES), 1)
    over_first = (((0,), (0,)), ((), ()))
    total = jnp.zeros((LANES, 8 * LANES), F32)
    for b in range(2):
        which = ids_f[rows_of(4 + b, PEERS, 8), :].astype(jnp.int32)
        chosen = (lane == which).astype(F32).astype(BF16)
        terms = jnp.concatenate(
            [in_f[rows_of(b * 8 + k, PEERS, 16), :] for k in range(8)], axis=1
        ).astype(BF16)
        total += lax.dot_general(chosen, terms, over_first, preferred_element_type=F32)
    for k in range(8):
        out_ref[rows_of(k, 32, 8), :] = total[:32, k * LANES:(k + 1) * LANES]


def unpack(in_ref, down_ref, up_ref, rows_f):
    for m, map_ref in ((0, up_ref), (1, down_ref)):
        for i in range(2):
            rows_f[rows_of(i, PEERS, 2), :] = in_ref[rows_of(2 * m + i, PEERS, 4), :]
        for c in range(BANDS):
            map_ref[:, c * LANES:(c + 1) * LANES] = rows_f[c * 8:(c + 1) * 8, :]


def call(kernel, outs, specs, scratch=(), cost=None, limit=40 * MIB):
    return pl.pallas_call(
        kernel,
        out_shape=[jax.ShapeDtypeStruct(shape, dtype) for shape, dtype in outs],
        in_specs=specs,
        out_specs=[VMEM] * len(outs),
        scratch_shapes=scratch,
        compiler_params=pltpu.CompilerParams(vmem_limit_bytes=limit),
        cost_estimate=cost,
    )


def swap(x):
    chunks = x.reshape(PEERS, x.shape[0] // PEERS, LANES)
    return lax.all_to_all(chunks, "dp", 0, 0, tiled=True).reshape(x.shape)


def from_peer(x, k):
    return lax.ppermute(x, "tensor", [(i, i ^ k) for i in range(4)])


def per_device(attn, output_gradient, down_weight, up_weight, adapter_of_row, lengths):
    width = attn.shape[1]
    me = lax.axis_index("tensor")
    me = me.astype(jnp.int32).reshape(1)
    (packed,) = call(
        pack_tables,
        [((8 * PEERS, LANES), BF16)],
        [ANY] * 3,
        [
            pltpu.VMEM((8, width), BF16),
            pltpu.VMEM((8, width), BF16),
            pltpu.VMEM((2, BLOCK), jnp.int32),
            pltpu.VMEM((2 * PEERS, LANES), F32),
            pltpu.VMEM((8 * PEERS, LANES), F32),
            pltpu.SemaphoreType.DMA((3,)),
        ],
        limit=56 * MIB,
    )(down_weight, up_weight, adapter_of_row.reshape(2, BLOCK))

    def cut(ks, flops):
        return call(
            functools.partial(cut_tokens, ks),
            [((64 * len(ks), width), BF16)],
            [SMEM, ANY, ANY],
            [pltpu.SemaphoreType.DMA((len(ks),))],
            cost=pl.CostEstimate(flops=flops, bytes_accessed=len(ks) << 19, transcendentals=0),
            limit=56 * MIB,
        )(me, output_gradient, packed)[0]

    far, near = cut((2, 3), 1000), cut((1,), 10 ** 10)
    live = (adapter_of_row >= 0) & (jnp.arange(2 * BLOCK, dtype=jnp.int32) < lengths[0])
    live = live.astype(F32).reshape(2, BLOCK)
    tables = swap(packed)
    tables, near = lax.optimization_barrier((tables, near))
    near, far = from_peer(near, 1), from_peer(far, 2)
    odd, live = lax.optimization_barrier((from_peer(far[64:], 1), live))
    pieces = [near, far, odd]
    (picked,) = call(
        pick_rows,
        [((16 * PEERS, LANES), BF16)],
        [VMEM],
        [pltpu.VMEM((8 * PEERS, LANES), F32), pltpu.VMEM((16 * PEERS, LANES), F32)],
    )(tables)
    picked = swap(picked)
    maps, grad, part = call(
        project,
        [((64, width), BF16), ((2 * BLOCK, width), BF16), ((32, 2 * BLOCK), F32)],
        [SMEM] + [VMEM] * 6,
    )(me, picked, attn, output_gradient, *pieces)
    parts = [part] + [from_peer(part, k) for k in (1, 2, 3)]
    ranks, terms = call(
        make_terms,
        [((32, 2 * BLOCK), BF16), ((16 * PEERS, LANES), BF16)],
        [VMEM] * 7,
    )(*parts, live, attn, grad)
    terms = swap(terms)
    (attention_gradient,) = call(
        go_back,
        [((2 * BLOCK, width), BF16)],
        [VMEM] * 2,
        cost=pl.CostEstimate(flops=2 * 32 * 256 * 2048, bytes_accessed=2 << 20, transcendentals=0),
    )(ranks, maps)
    (sums,) = call(
        add_up,
        [((4 * PEERS, LANES), F32)],
        [VMEM, VMEM],
        [pltpu.VMEM((16 * PEERS, LANES), F32), pltpu.VMEM((8 * PEERS, LANES), F32)],
    )(terms, tables)
    sums = swap(sums)
    grad_a, grad_b = call(
        unpack,
        [((8, width), F32), ((8, width), F32)],
        [VMEM],
        [pltpu.VMEM((2 * PEERS, LANES), F32)],
    )(sums)
    return attention_gradient, grad_a, grad_b


def solution(mesh):
    return jax.shard_map(
        per_device,
        mesh=mesh,
        in_specs=(
            P("dp", "tensor"),
            P(("dp", "tensor"), None),
            P("dp", "tensor"),
            P("dp", "tensor"),
            P("dp"),
            P("dp"),
        ),
        out_specs=(P("dp", "tensor"), P("dp", "tensor"), P("dp", "tensor")),
        check_vma=False,
    )
```

```python
import functools

import jax
import jax.numpy as jnp
from jax import lax
from jax.experimental import pallas as pl
from jax.experimental.pallas import tpu as pltpu
from jax.sharding import PartitionSpec as P

LANES = 128
BLOCK = 128
PEERS = 64
BANDS = 16
QUARTERS = 4

F32 = jnp.float32
BF16 = jnp.bfloat16

adapter_scale = 2.0

VMEM = pl.BlockSpec(memory_space=pltpu.VMEM)
ANY = pl.BlockSpec(memory_space=pl.ANY)
SMEM = pl.BlockSpec(memory_space=pltpu.SMEM)
MIB = 1024 * 1024


def rows_of(first, size, stride):
    return pl.ds(first, size, stride=stride)


def pack_tables(down_hbm, up_hbm, label_hbm, out_ref, down_ref, up_ref, label_ref, rows_f, out_f, sems):
    moves = ((label_hbm, label_ref), (down_hbm, down_ref), (up_hbm, up_ref))
    copies = [pltpu.make_async_copy(src, dst, sems.at[n]) for n, (src, dst) in enumerate(moves)]
    for copy in copies:
        copy.start()
    for b in range(2):
        out_f[rows_of(6 + b, PEERS, 8), :] = jnp.zeros((PEERS, LANES), F32)
    copies[0].wait()
    labels = label_ref[...]
    for b in range(2):
        which = jnp.maximum(labels[b:b + 1, 0:1], 0).astype(F32)
        out_f[rows_of(4 + b, PEERS, 8), :] = jnp.broadcast_to(which, (PEERS, LANES))
    for m, map_ref in enumerate((down_ref, up_ref)):
        copies[1 + m].wait()
        for c in range(BANDS):
            rows_f[c * 8:(c + 1) * 8, :] = map_ref[:, c * LANES:(c + 1) * LANES].astype(F32)
        for i in range(2):
            out_f[rows_of(2 * m + i, PEERS, 8), :] = rows_f[rows_of(i, PEERS, 2), :]
    out_ref[...] = out_f[...].astype(BF16)


def cut_tokens(ks, place_ref, grad_hbm, packed_hbm, out_ref, sems):
    width = out_ref.shape[1]
    copies = []
    for n, k in enumerate(ks):
        first = pl.multiple_of(lax.bitwise_xor(place_ref[0], k) * width, width)
        piece = out_ref.at[pl.ds(n * 64, 64), :]
        copies.append(pltpu.make_async_copy(grad_hbm.at[:, pl.ds(first, width)], piece, sems.at[n]))
    for copy in copies:
        copy.start()
    for copy in copies:
        copy.wait()


def pick_rows(in_ref, out_ref, in_f, out_f):
    in_f[...] = in_ref[...].astype(F32)
    table = jnp.concatenate([in_f[rows_of(k, PEERS, 8), :] for k in range(4)], axis=1).astype(BF16)
    lane = lax.broadcasted_iota(jnp.int32, (PEERS, LANES), 1)
    for b in range(2):
        which = in_f[rows_of(4 + b, PEERS, 8), :].astype(jnp.int32)
        for h in range(2):
            chosen = (lane == 2 * which + h).astype(F32).astype(BF16)[:, :PEERS]
            picked = jnp.dot(chosen, table, preferred_element_type=F32)
            for k in range(4):
                out_f[rows_of(b * 8 + h * 4 + k, PEERS, 16), :] = picked[:, k * LANES:(k + 1) * LANES]
    out_ref[...] = out_f[...].astype(BF16)


def project(place_ref, picked_ref, attn_ref, tokens_ref, one_ref, two_ref, three_ref, maps_ref, grad_ref, part_ref):
    me = place_ref[0]
    width = grad_ref.shape[1]
    own = tokens_ref[:, pl.ds(pl.multiple_of(me * width, width), width)]
    grad_ref[pl.ds(pl.multiple_of(me * 64, 64), 64), :] = own
    for k, piece in ((1, one_ref), (2, two_ref), (3, three_ref)):
        first = pl.multiple_of(lax.bitwise_xor(me, k) * 64, 64)
        grad_ref[pl.ds(first, 64), :] = piece[:64, :]
    for c in range(BANDS):
        rows = picked_ref[c * 64:(c + 1) * 64, :].astype(F32).reshape(QUARTERS, 2, 8, LANES)
        for b in range(2):
            maps_ref[b * 32:(b + 1) * 32, c * LANES:(c + 1) * LANES] = rows[:, b].reshape(32, LANES).astype(BF16)
    row = lax.broadcasted_iota(jnp.int32, (32, BLOCK), 0)
    over_last = (((1,), (1,)), ((), ()))
    for b in range(2):
        maps = maps_ref[b * 32:(b + 1) * 32, :]
        block = slice(b * BLOCK, (b + 1) * BLOCK)
        inner = lax.dot_general(maps, attn_ref[block, :], over_last, preferred_element_type=F32)
        outer = lax.dot_general(maps, grad_ref[block, :], over_last, preferred_element_type=F32)
        part_ref[:, block] = jnp.where((row & 2) == 0, inner, outer)


def make_terms(own_ref, one_ref, two_ref, three_ref, live_ref, attn_ref, grad_ref, ranks_ref, term_ref):
    total = (own_ref[...] + one_ref[...]) + (two_ref[...] + three_ref[...])
    row = lax.broadcasted_iota(jnp.int32, (32, LANES), 0)
    terms = []
    for b in range(2):
        block = slice(b * BLOCK, (b + 1) * BLOCK)
        ranks = jnp.where(live_ref[b:b + 1, :] > 0, total[:, block], 0.0).astype(BF16)
        ranks_ref[:, block] = ranks
        down = jnp.dot(ranks, attn_ref[block, :], preferred_element_type=F32)
        up = jnp.dot(ranks, grad_ref[block, :], preferred_element_type=F32)
        terms.append((down, up))
    for c in range(BANDS):
        band = slice(c * LANES, (c + 1) * LANES)
        both = [
            adapter_scale * jnp.where((row & 2) == 0, up[:, band], down[:, band])
            for down, up in terms
        ]
        for q in range(QUARTERS):
            pair = jnp.concatenate([one[q * 8:(q + 1) * 8] for one in both], axis=0)
            term_ref[c * 64 + q * 16:c * 64 + (q + 1) * 16, :] = pair.astype(BF16)


def go_back(ranks_ref, maps_ref, back_ref):
    row = lax.broadcasted_iota(jnp.int32, (32, BLOCK), 0)
    over_first = (((0,), (0,)), ((), ()))
    for b in range(2):
        block = slice(b * BLOCK, (b + 1) * BLOCK)
        shifted = pltpu.roll(ranks_ref[:, block].astype(F32), 30, 0)
        outer = jnp.where((row & 2) == 0, shifted, 0.0).astype(BF16)
        back = lax.dot_general(outer, maps_ref[b * 32:(b + 1) * 32, :], over_first, preferred_element_type=F32)
        back_ref[block, :] = (adapter_scale * back).astype(BF16)


def add_up(in_ref, ids_ref, out_ref, in_f, ids_f):
    in_f[...] = in_ref[...].astype(F32)
    ids_f[...] = ids_ref[...].astype(F32)
    lane = lax.broadcasted_iota(jnp.int32, (PEERS, LANES), 1)
    over_first = (((0,), (0,)), ((), ()))
    total = jnp.zeros((LANES, 8 * LANES), F32)
    for b in range(2):
        which = ids_f[rows_of(4 + b, PEERS, 8), :].astype(jnp.int32)
        chosen = (lane == which).astype(F32).astype(BF16)
        terms = jnp.concatenate(
            [in_f[rows_of(b * 8 + k, PEERS, 16), :] for k in range(8)], axis=1
        ).astype(BF16)
        total += lax.dot_general(chosen, terms, over_first, preferred_element_type=F32)
    for k in range(8):
        out_ref[rows_of(k, 32, 8), :] = total[:32, k * LANES:(k + 1) * LANES]


def unpack(in_ref, down_ref, up_ref, rows_f):
    for m, map_ref in ((0, up_ref), (1, down_ref)):
        for i in range(2):
            rows_f[rows_of(i, PEERS, 2), :] = in_ref[rows_of(2 * m + i, PEERS, 4), :]
        for c in range(BANDS):
            map_ref[:, c * LANES:(c + 1) * LANES] = rows_f[c * 8:(c + 1) * 8, :]


def call(kernel, outs, specs, scratch=(), cost=None, limit=40 * MIB):
    return pl.pallas_call(
        kernel,
        out_shape=[jax.ShapeDtypeStruct(shape, dtype) for shape, dtype in outs],
        in_specs=specs,
        out_specs=[VMEM] * len(outs),
        scratch_shapes=scratch,
        compiler_params=pltpu.CompilerParams(vmem_limit_bytes=limit),
        cost_estimate=cost,
    )


def swap(x):
    chunks = x.reshape(PEERS, x.shape[0] // PEERS, LANES)
    return lax.all_to_all(chunks, "dp", 0, 0, tiled=True).reshape(x.shape)


def from_peer(x, k):
    return lax.ppermute(x, "tensor", [(i, i ^ k) for i in range(4)])


def per_device(attn, output_gradient, down_weight, up_weight, adapter_of_row, lengths):
    width = attn.shape[1]
    me = lax.axis_index("tensor")
    me = me.astype(jnp.int32).reshape(1)
    (packed,) = call(
        pack_tables,
        [((8 * PEERS, LANES), BF16)],
        [ANY] * 3,
        [
            pltpu.VMEM((8, width), BF16),
            pltpu.VMEM((8, width), BF16),
            pltpu.VMEM((2, BLOCK), jnp.int32),
            pltpu.VMEM((2 * PEERS, LANES), F32),
            pltpu.VMEM((8 * PEERS, LANES), F32),
            pltpu.SemaphoreType.DMA((3,)),
        ],
        limit=56 * MIB,
    )(down_weight, up_weight, adapter_of_row.reshape(2, BLOCK))

    def cut(ks, flops):
        return call(
            functools.partial(cut_tokens, ks),
            [((64 * len(ks), width), BF16)],
            [SMEM, ANY, ANY],
            [pltpu.SemaphoreType.DMA((len(ks),))],
            cost=pl.CostEstimate(flops=flops, bytes_accessed=len(ks) << 19, transcendentals=0),
            limit=56 * MIB,
        )(me, output_gradient, packed)[0]

    far, near = cut((2, 3), 1000), cut((1,), 10 ** 10)
    live = (adapter_of_row >= 0) & (jnp.arange(2 * BLOCK, dtype=jnp.int32) < lengths[0])
    live = live.astype(F32).reshape(2, BLOCK)
    tables = swap(packed)
    tables, near = lax.optimization_barrier((tables, near))
    near, far = from_peer(near, 1), from_peer(far, 2)
    odd, live = lax.optimization_barrier((from_peer(far[64:], 1), live))
    pieces = [near, far, odd]
    (picked,) = call(
        pick_rows,
        [((16 * PEERS, LANES), BF16)],
        [VMEM],
        [pltpu.VMEM((8 * PEERS, LANES), F32), pltpu.VMEM((16 * PEERS, LANES), F32)],
    )(tables)
    picked = swap(picked)
    maps, grad, part = call(
        project,
        [((64, width), BF16), ((2 * BLOCK, width), BF16), ((32, 2 * BLOCK), F32)],
        [SMEM] + [VMEM] * 6,
    )(me, picked, attn, output_gradient, *pieces)
    across, beside = from_peer(part, 2), from_peer(part, 1)
    parts = [part, beside, across, from_peer(across, 1)]
    ranks, terms = call(
        make_terms,
        [((32, 2 * BLOCK), BF16), ((16 * PEERS, LANES), BF16)],
        [VMEM] * 7,
    )(*parts, live, attn, grad)
    terms = swap(terms)
    (attention_gradient,) = call(
        go_back,
        [((2 * BLOCK, width), BF16)],
        [VMEM] * 2,
        cost=pl.CostEstimate(flops=2 * 32 * 256 * 2048, bytes_accessed=2 << 20, transcendentals=0),
    )(ranks, maps)
    (sums,) = call(
        add_up,
        [((4 * PEERS, LANES), F32)],
        [VMEM, VMEM],
        [pltpu.VMEM((16 * PEERS, LANES), F32), pltpu.VMEM((8 * PEERS, LANES), F32)],
    )(terms, tables)
    sums = swap(sums)
    grad_a, grad_b = call(
        unpack,
        [((8, width), F32), ((8, width), F32)],
        [VMEM],
        [pltpu.VMEM((2 * PEERS, LANES), F32)],
    )(sums)
    return attention_gradient, grad_a, grad_b


def solution(mesh):
    return jax.shard_map(
        per_device,
        mesh=mesh,
        in_specs=(
            P("dp", "tensor"),
            P(("dp", "tensor"), None),
            P("dp", "tensor"),
            P("dp", "tensor"),
            P("dp"),
            P("dp"),
        ),
        out_specs=(P("dp", "tensor"), P("dp", "tensor"), P("dp", "tensor")),
        check_vma=False,
    )
```

```python
import jax
import jax.numpy as jnp
from jax import lax
from jax.experimental import pallas as pl
from jax.experimental.pallas import tpu as pltpu
from jax.sharding import PartitionSpec as P

LANES = 128
BLOCK = 128
PEERS = 64
BANDS = 16
QUARTERS = 4

F32 = jnp.float32
BF16 = jnp.bfloat16

adapter_scale = 2.0

VMEM = pl.BlockSpec(memory_space=pltpu.VMEM)
ANY = pl.BlockSpec(memory_space=pl.ANY)
SMEM = pl.BlockSpec(memory_space=pltpu.SMEM)
MIB = 1024 * 1024


def rows_of(first, size, stride):
    return pl.ds(first, size, stride=stride)


def pack_tables(down_hbm, up_hbm, label_hbm, out_ref, down_ref, up_ref, label_ref, rows_f, out_f, sems):
    moves = ((label_hbm, label_ref), (down_hbm, down_ref), (up_hbm, up_ref))
    copies = [pltpu.make_async_copy(src, dst, sems.at[n]) for n, (src, dst) in enumerate(moves)]
    for copy in copies:
        copy.start()
    for b in range(2):
        out_f[rows_of(6 + b, PEERS, 8), :] = jnp.zeros((PEERS, LANES), F32)
    copies[0].wait()
    labels = label_ref[...]
    for b in range(2):
        which = jnp.maximum(labels[b:b + 1, 0:1], 0).astype(F32)
        out_f[rows_of(4 + b, PEERS, 8), :] = jnp.broadcast_to(which, (PEERS, LANES))
    for m, map_ref in enumerate((down_ref, up_ref)):
        copies[1 + m].wait()
        for c in range(BANDS):
            rows_f[c * 8:(c + 1) * 8, :] = map_ref[:, c * LANES:(c + 1) * LANES].astype(F32)
        for i in range(2):
            out_f[rows_of(2 * m + i, PEERS, 8), :] = rows_f[rows_of(i, PEERS, 2), :]
    out_ref[...] = out_f[...].astype(BF16)


def cut_tokens(place_ref, grad_hbm, packed_hbm, near_ref, far_ref, sems):
    width = near_ref.shape[1]
    copies = []
    for k, piece in ((2, far_ref.at[pl.ds(0, 64), :]), (3, far_ref.at[pl.ds(64, 64), :]), (1, near_ref)):
        first = pl.multiple_of(lax.bitwise_xor(place_ref[0], k) * width, width)
        copies.append(pltpu.make_async_copy(grad_hbm.at[:, pl.ds(first, width)], piece, sems.at[k - 1]))
    for copy in copies:
        copy.start()
    for copy in copies:
        copy.wait()


def copy_place(place_ref, out_ref):
    out_ref[0] = place_ref[0]


def pick_rows(in_ref, out_ref, in_f, out_f):
    in_f[...] = in_ref[...].astype(F32)
    table = jnp.concatenate([in_f[rows_of(k, PEERS, 8), :] for k in range(4)], axis=1).astype(BF16)
    lane = lax.broadcasted_iota(jnp.int32, (PEERS, LANES), 1)
    for b in range(2):
        which = in_f[rows_of(4 + b, PEERS, 8), :].astype(jnp.int32)
        for h in range(2):
            chosen = (lane == 2 * which + h).astype(F32).astype(BF16)[:, :PEERS]
            picked = jnp.dot(chosen, table, preferred_element_type=F32)
            for k in range(4):
                out_f[rows_of(b * 8 + h * 4 + k, PEERS, 16), :] = picked[:, k * LANES:(k + 1) * LANES]
    out_ref[...] = out_f[...].astype(BF16)


def project(
    place_ref, order_ref, picked_ref, attn_ref, tokens_ref, one_ref, two_ref, three_ref, maps_ref, grad_ref, part_ref
):
    me = place_ref[0]
    width = grad_ref.shape[1]
    own = tokens_ref[:, pl.ds(pl.multiple_of(me * width, width), width)]
    grad_ref[pl.ds(pl.multiple_of(me * 64, 64), 64), :] = own
    for k, piece in ((1, one_ref), (2, two_ref), (3, three_ref)):
        first = pl.multiple_of(lax.bitwise_xor(me, k) * 64, 64)
        grad_ref[pl.ds(first, 64), :] = piece[:64, :]
    for c in range(BANDS):
        rows = picked_ref[c * 64:(c + 1) * 64, :].astype(F32).reshape(QUARTERS, 2, 8, LANES)
        for b in range(2):
            maps_ref[b * 32:(b + 1) * 32, c * LANES:(c + 1) * LANES] = rows[:, b].reshape(32, LANES).astype(BF16)
    row = lax.broadcasted_iota(jnp.int32, (32, BLOCK), 0)
    over_last = (((1,), (1,)), ((), ()))
    for b in range(2):
        maps = maps_ref[b * 32:(b + 1) * 32, :]
        block = slice(b * BLOCK, (b + 1) * BLOCK)
        inner = lax.dot_general(maps, attn_ref[block, :], over_last, preferred_element_type=F32)
        outer = lax.dot_general(maps, grad_ref[block, :], over_last, preferred_element_type=F32)
        part_ref[:, block] = jnp.where((row & 2) == 0, inner, outer)


def make_terms(own_ref, one_ref, two_ref, three_ref, live_ref, attn_ref, grad_ref, ranks_ref, term_ref):
    total = (own_ref[...] + one_ref[...]) + (two_ref[...] + three_ref[...])
    row = lax.broadcasted_iota(jnp.int32, (32, LANES), 0)
    terms = []
    for b in range(2):
        block = slice(b * BLOCK, (b + 1) * BLOCK)
        ranks = jnp.where(live_ref[b:b + 1, :] > 0, total[:, block], 0.0).astype(BF16)
        ranks_ref[:, block] = ranks
        down = jnp.dot(ranks, attn_ref[block, :], preferred_element_type=F32)
        up = jnp.dot(ranks, grad_ref[block, :], preferred_element_type=F32)
        terms.append((down, up))
    for c in range(BANDS):
        band = slice(c * LANES, (c + 1) * LANES)
        both = [
            adapter_scale * jnp.where((row & 2) == 0, up[:, band], down[:, band])
            for down, up in terms
        ]
        for q in range(QUARTERS):
            pair = jnp.concatenate([one[q * 8:(q + 1) * 8] for one in both], axis=0)
            term_ref[c * 64 + q * 16:c * 64 + (q + 1) * 16, :] = pair.astype(BF16)


def go_back(ranks_ref, maps_ref, back_ref):
    row = lax.broadcasted_iota(jnp.int32, (32, BLOCK), 0)
    over_first = (((0,), (0,)), ((), ()))
    for b in range(2):
        block = slice(b * BLOCK, (b + 1) * BLOCK)
        shifted = pltpu.roll(ranks_ref[:, block].astype(F32), 30, 0)
        outer = jnp.where((row & 2) == 0, shifted, 0.0).astype(BF16)
        back = lax.dot_general(outer, maps_ref[b * 32:(b + 1) * 32, :], over_first, preferred_element_type=F32)
        back_ref[block, :] = (adapter_scale * back).astype(BF16)


def add_up(in_ref, ids_ref, out_ref, in_f, ids_f):
    in_f[...] = in_ref[...].astype(F32)
    ids_f[...] = ids_ref[...].astype(F32)
    lane = lax.broadcasted_iota(jnp.int32, (PEERS, LANES), 1)
    over_first = (((0,), (0,)), ((), ()))
    total = jnp.zeros((LANES, 8 * LANES), F32)
    for b in range(2):
        which = ids_f[rows_of(4 + b, PEERS, 8), :].astype(jnp.int32)
        chosen = (lane == which).astype(F32).astype(BF16)
        terms = jnp.concatenate(
            [in_f[rows_of(b * 8 + k, PEERS, 16), :] for k in range(8)], axis=1
        ).astype(BF16)
        total += lax.dot_general(chosen, terms, over_first, preferred_element_type=F32)
    for k in range(8):
        out_ref[rows_of(k, 32, 8), :] = total[:32, k * LANES:(k + 1) * LANES]


def unpack(in_ref, down_ref, up_ref, rows_f):
    for m, map_ref in ((0, up_ref), (1, down_ref)):
        for i in range(2):
            rows_f[rows_of(i, PEERS, 2), :] = in_ref[rows_of(2 * m + i, PEERS, 4), :]
        for c in range(BANDS):
            map_ref[:, c * LANES:(c + 1) * LANES] = rows_f[c * 8:(c + 1) * 8, :]


def call(kernel, outs, specs, scratch=(), cost=None, limit=40 * MIB):
    return pl.pallas_call(
        kernel,
        out_shape=[jax.ShapeDtypeStruct(shape, dtype) for shape, dtype in outs],
        in_specs=specs,
        out_specs=[VMEM] * len(outs),
        scratch_shapes=scratch,
        compiler_params=pltpu.CompilerParams(vmem_limit_bytes=limit),
        cost_estimate=cost,
    )


def swap(x):
    chunks = x.reshape(PEERS, x.shape[0] // PEERS, LANES)
    return lax.all_to_all(chunks, "dp", 0, 0, tiled=True).reshape(x.shape)


def from_peer(x, k):
    return lax.ppermute(x, "tensor", [(i, i ^ k) for i in range(4)])


def per_device(attn, output_gradient, down_weight, up_weight, adapter_of_row, lengths):
    width = attn.shape[1]
    me = lax.axis_index("tensor")
    me = me.astype(jnp.int32).reshape(1)
    (packed,) = call(
        pack_tables,
        [((8 * PEERS, LANES), BF16)],
        [ANY] * 3,
        [
            pltpu.VMEM((8, width), BF16),
            pltpu.VMEM((8, width), BF16),
            pltpu.VMEM((2, BLOCK), jnp.int32),
            pltpu.VMEM((2 * PEERS, LANES), F32),
            pltpu.VMEM((8 * PEERS, LANES), F32),
            pltpu.SemaphoreType.DMA((3,)),
        ],
        limit=56 * MIB,
    )(down_weight, up_weight, adapter_of_row.reshape(2, BLOCK))
    near, far = call(
        cut_tokens,
        [((64, width), BF16), ((128, width), BF16)],
        [SMEM, ANY, ANY],
        [pltpu.SemaphoreType.DMA((3,))],
        limit=56 * MIB,
    )(me, output_gradient, packed)
    order = pl.pallas_call(
        copy_place,
        out_shape=jax.ShapeDtypeStruct((1,), jnp.int32),
        in_specs=[SMEM],
        out_specs=SMEM,
        cost_estimate=pl.CostEstimate(flops=10 ** 10, bytes_accessed=8, transcendentals=0),
    )(me)
    live = (adapter_of_row >= 0) & (jnp.arange(2 * BLOCK, dtype=jnp.int32) < lengths[0])
    live = live.astype(F32).reshape(2, BLOCK)
    tables = swap(packed)
    tables, order = lax.optimization_barrier((tables, order))
    near, far = from_peer(near, 1), from_peer(far, 2)
    odd, live = lax.optimization_barrier((from_peer(far[64:], 1), live))
    pieces = [near, far, odd]
    (picked,) = call(
        pick_rows,
        [((16 * PEERS, LANES), BF16)],
        [VMEM],
        [pltpu.VMEM((8 * PEERS, LANES), F32), pltpu.VMEM((16 * PEERS, LANES), F32)],
    )(tables)
    picked = swap(picked)
    maps, grad, part = call(
        project,
        [((64, width), BF16), ((2 * BLOCK, width), BF16), ((32, 2 * BLOCK), F32)],
        [SMEM, ANY] + [VMEM] * 6,
    )(me, order, picked, attn, output_gradient, *pieces)
    parts = [part] + [from_peer(part, k) for k in (1, 2, 3)]
    ranks, terms = call(
        make_terms,
        [((32, 2 * BLOCK), BF16), ((16 * PEERS, LANES), BF16)],
        [VMEM] * 7,
    )(*parts, live, attn, grad)
    terms = swap(terms)
    (attention_gradient,) = call(
        go_back,
        [((2 * BLOCK, width), BF16)],
        [VMEM] * 2,
        cost=pl.CostEstimate(flops=2 * 32 * 256 * 2048, bytes_accessed=2 << 20, transcendentals=0),
    )(ranks, maps)
    (sums,) = call(
        add_up,
        [((4 * PEERS, LANES), F32)],
        [VMEM, VMEM],
        [pltpu.VMEM((16 * PEERS, LANES), F32), pltpu.VMEM((8 * PEERS, LANES), F32)],
    )(terms, tables)
    sums = swap(sums)
    grad_a, grad_b = call(
        unpack,
        [((8, width), F32), ((8, width), F32)],
        [VMEM],
        [pltpu.VMEM((2 * PEERS, LANES), F32)],
    )(sums)
    return attention_gradient, grad_a, grad_b


def solution(mesh):
    return jax.shard_map(
        per_device,
        mesh=mesh,
        in_specs=(
            P("dp", "tensor"),
            P(("dp", "tensor"), None),
            P("dp", "tensor"),
            P("dp", "tensor"),
            P("dp"),
            P("dp"),
        ),
        out_specs=(P("dp", "tensor"), P("dp", "tensor"), P("dp", "tensor")),
        check_vma=False,
    )
```

```python
import jax
import jax.numpy as jnp
from jax import lax
from jax.experimental import pallas as pl
from jax.experimental.pallas import tpu as pltpu
from jax.sharding import PartitionSpec as P

LANES = 128
BLOCK = 128
PEERS = 64
BANDS = 16
QUARTERS = 4

F32 = jnp.float32
BF16 = jnp.bfloat16

adapter_scale = 2.0

VMEM = pl.BlockSpec(memory_space=pltpu.VMEM)
ANY = pl.BlockSpec(memory_space=pl.ANY)
SMEM = pl.BlockSpec(memory_space=pltpu.SMEM)
MIB = 1024 * 1024


def rows_of(first, size, stride):
    return pl.ds(first, size, stride=stride)


def pack_tables(down_hbm, up_hbm, label_hbm, out_ref, down_ref, up_ref, label_ref, rows_f, out_f, sems):
    moves = ((label_hbm, label_ref), (down_hbm, down_ref), (up_hbm, up_ref))
    copies = [pltpu.make_async_copy(src, dst, sems.at[n]) for n, (src, dst) in enumerate(moves)]
    for copy in copies:
        copy.start()
    for b in range(2):
        out_f[rows_of(6 + b, PEERS, 8), :] = jnp.zeros((PEERS, LANES), F32)
    copies[0].wait()
    labels = label_ref[...]
    for b in range(2):
        which = jnp.maximum(labels[b:b + 1, 0:1], 0).astype(F32)
        out_f[rows_of(4 + b, PEERS, 8), :] = jnp.broadcast_to(which, (PEERS, LANES))
    for m, map_ref in enumerate((down_ref, up_ref)):
        copies[1 + m].wait()
        for c in range(BANDS):
            rows_f[c * 8:(c + 1) * 8, :] = map_ref[:, c * LANES:(c + 1) * LANES].astype(F32)
        for i in range(2):
            out_f[rows_of(2 * m + i, PEERS, 8), :] = rows_f[rows_of(i, PEERS, 2), :]
    out_ref[...] = out_f[...].astype(BF16)


def cut_tokens(place_ref, grad_hbm, packed_hbm, near_ref, far_ref, sems):
    width = near_ref.shape[1]
    copies = []
    for k, piece in ((2, far_ref.at[pl.ds(0, 64), :]), (3, far_ref.at[pl.ds(64, 64), :]), (1, near_ref)):
        first = pl.multiple_of(lax.bitwise_xor(place_ref[0], k) * width, width)
        copies.append(pltpu.make_async_copy(grad_hbm.at[:, pl.ds(first, width)], piece, sems.at[k - 1]))
    for copy in copies:
        copy.start()
    for copy in copies:
        copy.wait()


def copy_place(place_ref, out_ref):
    out_ref[0] = place_ref[0]


def pick_rows(in_ref, out_ref, in_f, out_f):
    in_f[...] = in_ref[...].astype(F32)
    table = jnp.concatenate([in_f[rows_of(k, PEERS, 8), :] for k in range(4)], axis=1).astype(BF16)
    lane = lax.broadcasted_iota(jnp.int32, (PEERS, LANES), 1)
    for b in range(2):
        which = in_f[rows_of(4 + b, PEERS, 8), :].astype(jnp.int32)
        for h in range(2):
            chosen = (lane == 2 * which + h).astype(F32).astype(BF16)[:, :PEERS]
            picked = jnp.dot(chosen, table, preferred_element_type=F32)
            for k in range(4):
                out_f[rows_of(b * 8 + h * 4 + k, PEERS, 16), :] = picked[:, k * LANES:(k + 1) * LANES]
    out_ref[...] = out_f[...].astype(BF16)


def project(place_ref, picked_ref, attn_ref, tokens_ref, one_ref, two_ref, three_ref, maps_ref, grad_ref, part_ref):
    me = place_ref[0]
    width = grad_ref.shape[1]
    own = tokens_ref[:, pl.ds(pl.multiple_of(me * width, width), width)]
    grad_ref[pl.ds(pl.multiple_of(me * 64, 64), 64), :] = own
    for k, piece in ((1, one_ref), (2, two_ref), (3, three_ref)):
        first = pl.multiple_of(lax.bitwise_xor(me, k) * 64, 64)
        grad_ref[pl.ds(first, 64), :] = piece[:64, :]
    for c in range(BANDS):
        rows = picked_ref[c * 64:(c + 1) * 64, :].astype(F32).reshape(QUARTERS, 2, 8, LANES)
        for b in range(2):
            maps_ref[b * 32:(b + 1) * 32, c * LANES:(c + 1) * LANES] = rows[:, b].reshape(32, LANES).astype(BF16)
    row = lax.broadcasted_iota(jnp.int32, (32, BLOCK), 0)
    over_last = (((1,), (1,)), ((), ()))
    for b in range(2):
        maps = maps_ref[b * 32:(b + 1) * 32, :]
        block = slice(b * BLOCK, (b + 1) * BLOCK)
        inner = lax.dot_general(maps, attn_ref[block, :], over_last, preferred_element_type=F32)
        outer = lax.dot_general(maps, grad_ref[block, :], over_last, preferred_element_type=F32)
        part_ref[:, block] = jnp.where((row & 2) == 0, inner, outer)


def make_terms(own_ref, one_ref, two_ref, three_ref, live_ref, attn_ref, grad_ref, ranks_ref, term_ref):
    total = (own_ref[...] + one_ref[...]) + (two_ref[...] + three_ref[...])
    row = lax.broadcasted_iota(jnp.int32, (32, LANES), 0)
    terms = []
    for b in range(2):
        block = slice(b * BLOCK, (b + 1) * BLOCK)
        ranks = jnp.where(live_ref[b:b + 1, :] > 0, total[:, block], 0.0).astype(BF16)
        ranks_ref[:, block] = ranks
        down = jnp.dot(ranks, attn_ref[block, :], preferred_element_type=F32)
        up = jnp.dot(ranks, grad_ref[block, :], preferred_element_type=F32)
        terms.append((down, up))
    for c in range(BANDS):
        band = slice(c * LANES, (c + 1) * LANES)
        both = [
            adapter_scale * jnp.where((row & 2) == 0, up[:, band], down[:, band])
            for down, up in terms
        ]
        for q in range(QUARTERS):
            pair = jnp.concatenate([one[q * 8:(q + 1) * 8] for one in both], axis=0)
            term_ref[c * 64 + q * 16:c * 64 + (q + 1) * 16, :] = pair.astype(BF16)


def go_back(order_ref, ranks_ref, maps_ref, back_ref):
    row = lax.broadcasted_iota(jnp.int32, (32, BLOCK), 0)
    over_first = (((0,), (0,)), ((), ()))
    for b in range(2):
        block = slice(b * BLOCK, (b + 1) * BLOCK)
        shifted = pltpu.roll(ranks_ref[:, block].astype(F32), 30, 0)
        outer = jnp.where((row & 2) == 0, shifted, 0.0).astype(BF16)
        back = lax.dot_general(outer, maps_ref[b * 32:(b + 1) * 32, :], over_first, preferred_element_type=F32)
        back_ref[block, :] = (adapter_scale * back).astype(BF16)


def add_up(in_ref, ids_ref, out_ref, in_f, ids_f):
    in_f[...] = in_ref[...].astype(F32)
    ids_f[...] = ids_ref[...].astype(F32)
    lane = lax.broadcasted_iota(jnp.int32, (PEERS, LANES), 1)
    over_first = (((0,), (0,)), ((), ()))
    total = jnp.zeros((LANES, 8 * LANES), F32)
    for b in range(2):
        which = ids_f[rows_of(4 + b, PEERS, 8), :].astype(jnp.int32)
        chosen = (lane == which).astype(F32).astype(BF16)
        terms = jnp.concatenate(
            [in_f[rows_of(b * 8 + k, PEERS, 16), :] for k in range(8)], axis=1
        ).astype(BF16)
        total += lax.dot_general(chosen, terms, over_first, preferred_element_type=F32)
    for k in range(8):
        out_ref[rows_of(k, 32, 8), :] = total[:32, k * LANES:(k + 1) * LANES]


def unpack(in_ref, down_ref, up_ref, rows_f):
    for m, map_ref in ((0, up_ref), (1, down_ref)):
        for i in range(2):
            rows_f[rows_of(i, PEERS, 2), :] = in_ref[rows_of(2 * m + i, PEERS, 4), :]
        for c in range(BANDS):
            map_ref[:, c * LANES:(c + 1) * LANES] = rows_f[c * 8:(c + 1) * 8, :]


def call(kernel, outs, specs, scratch=(), cost=None, limit=40 * MIB):
    return pl.pallas_call(
        kernel,
        out_shape=[jax.ShapeDtypeStruct(shape, dtype) for shape, dtype in outs],
        in_specs=specs,
        out_specs=[VMEM] * len(outs),
        scratch_shapes=scratch,
        compiler_params=pltpu.CompilerParams(vmem_limit_bytes=limit),
        cost_estimate=cost,
    )


def swap(x):
    chunks = x.reshape(PEERS, x.shape[0] // PEERS, LANES)
    return lax.all_to_all(chunks, "dp", 0, 0, tiled=True).reshape(x.shape)


def from_peer(x, k):
    return lax.ppermute(x, "tensor", [(i, i ^ k) for i in range(4)])


def per_device(attn, output_gradient, down_weight, up_weight, adapter_of_row, lengths):
    width = attn.shape[1]
    me = lax.axis_index("tensor")
    me = me.astype(jnp.int32).reshape(1)
    (packed,) = call(
        pack_tables,
        [((8 * PEERS, LANES), BF16)],
        [ANY] * 3,
        [
            pltpu.VMEM((8, width), BF16),
            pltpu.VMEM((8, width), BF16),
            pltpu.VMEM((2, BLOCK), jnp.int32),
            pltpu.VMEM((2 * PEERS, LANES), F32),
            pltpu.VMEM((8 * PEERS, LANES), F32),
            pltpu.SemaphoreType.DMA((3,)),
        ],
        limit=56 * MIB,
    )(down_weight, up_weight, adapter_of_row.reshape(2, BLOCK))
    near, far = call(
        cut_tokens,
        [((64, width), BF16), ((128, width), BF16)],
        [SMEM, ANY, ANY],
        [pltpu.SemaphoreType.DMA((3,))],
        limit=56 * MIB,
    )(me, output_gradient, packed)
    order = pl.pallas_call(
        copy_place,
        out_shape=jax.ShapeDtypeStruct((1,), jnp.int32),
        in_specs=[SMEM],
        out_specs=SMEM,
        cost_estimate=pl.CostEstimate(flops=10 ** 10, bytes_accessed=8, transcendentals=0),
    )(me)
    live = (adapter_of_row >= 0) & (jnp.arange(2 * BLOCK, dtype=jnp.int32) < lengths[0])
    live = live.astype(F32).reshape(2, BLOCK)
    tables = swap(packed)
    tables, order = lax.optimization_barrier((tables, order))
    near, far = from_peer(near, 1), from_peer(far, 2)
    odd, live = lax.optimization_barrier((from_peer(far[64:], 1), live))
    pieces = [near, far, odd]
    (picked,) = call(
        pick_rows,
        [((16 * PEERS, LANES), BF16)],
        [VMEM],
        [pltpu.VMEM((8 * PEERS, LANES), F32), pltpu.VMEM((16 * PEERS, LANES), F32)],
    )(tables)
    picked = swap(picked)
    maps, grad, part = call(
        project,
        [((64, width), BF16), ((2 * BLOCK, width), BF16), ((32, 2 * BLOCK), F32)],
        [SMEM] + [VMEM] * 6,
    )(me, picked, attn, output_gradient, *pieces)
    parts = [part] + [from_peer(part, k) for k in (1, 2, 3)]
    ranks, terms = call(
        make_terms,
        [((32, 2 * BLOCK), BF16), ((16 * PEERS, LANES), BF16)],
        [VMEM] * 7,
    )(*parts, live, attn, grad)
    terms = swap(terms)
    (attention_gradient,) = call(
        go_back,
        [((2 * BLOCK, width), BF16)],
        [ANY] + [VMEM] * 2,
        cost=pl.CostEstimate(flops=2 * 32 * 256 * 2048, bytes_accessed=2 << 20, transcendentals=0),
    )(order, ranks, maps)
    (sums,) = call(
        add_up,
        [((4 * PEERS, LANES), F32)],
        [VMEM, VMEM],
        [pltpu.VMEM((16 * PEERS, LANES), F32), pltpu.VMEM((8 * PEERS, LANES), F32)],
    )(terms, tables)
    sums = swap(sums)
    grad_a, grad_b = call(
        unpack,
        [((8, width), F32), ((8, width), F32)],
        [VMEM],
        [pltpu.VMEM((2 * PEERS, LANES), F32)],
    )(sums)
    return attention_gradient, grad_a, grad_b


def solution(mesh):
    return jax.shard_map(
        per_device,
        mesh=mesh,
        in_specs=(
            P("dp", "tensor"),
            P(("dp", "tensor"), None),
            P("dp", "tensor"),
            P("dp", "tensor"),
            P("dp"),
            P("dp"),
        ),
        out_specs=(P("dp", "tensor"), P("dp", "tensor"), P("dp", "tensor")),
        check_vma=False,
    )
```

```python
import jax
import jax.numpy as jnp
from jax import lax
from jax.experimental import pallas as pl
from jax.experimental.pallas import tpu as pltpu
from jax.sharding import PartitionSpec as P

LANES = 128
BLOCK = 128
PEERS = 64
BANDS = 16
QUARTERS = 4

F32 = jnp.float32
BF16 = jnp.bfloat16

adapter_scale = 2.0

VMEM = pl.BlockSpec(memory_space=pltpu.VMEM)
ANY = pl.BlockSpec(memory_space=pl.ANY)
SMEM = pl.BlockSpec(memory_space=pltpu.SMEM)
MIB = 1024 * 1024


def rows_of(first, size, stride):
    return pl.ds(first, size, stride=stride)


def pack_tables(down_hbm, up_hbm, label_hbm, out_ref, down_ref, up_ref, label_ref, rows_f, out_f, sems):
    moves = ((label_hbm, label_ref), (down_hbm, down_ref), (up_hbm, up_ref))
    copies = [pltpu.make_async_copy(src, dst, sems.at[n]) for n, (src, dst) in enumerate(moves)]
    for copy in copies:
        copy.start()
    for b in range(2):
        out_f[rows_of(6 + b, PEERS, 8), :] = jnp.zeros((PEERS, LANES), F32)
    copies[0].wait()
    labels = label_ref[...]
    for b in range(2):
        which = jnp.maximum(labels[b:b + 1, 0:1], 0).astype(F32)
        out_f[rows_of(4 + b, PEERS, 8), :] = jnp.broadcast_to(which, (PEERS, LANES))
    for m, map_ref in enumerate((down_ref, up_ref)):
        copies[1 + m].wait()
        for c in range(BANDS):
            rows_f[c * 8:(c + 1) * 8, :] = map_ref[:, c * LANES:(c + 1) * LANES].astype(F32)
        for i in range(2):
            out_f[rows_of(2 * m + i, PEERS, 8), :] = rows_f[rows_of(i, PEERS, 2), :]
    out_ref[...] = out_f[...].astype(BF16)


def cut_tokens(place_ref, grad_hbm, packed_hbm, near_ref, far_ref, sems):
    width = near_ref.shape[1]
    copies = []
    for k, piece in ((2, far_ref.at[pl.ds(0, 64), :]), (3, far_ref.at[pl.ds(64, 64), :]), (1, near_ref)):
        first = pl.multiple_of(lax.bitwise_xor(place_ref[0], k) * width, width)
        copies.append(pltpu.make_async_copy(grad_hbm.at[:, pl.ds(first, width)], piece, sems.at[k - 1]))
    for copy in copies:
        copy.start()
    for copy in copies:
        copy.wait()


def copy_place(place_ref, out_ref):
    out_ref[...] = jnp.full(out_ref.shape, place_ref[0], jnp.int32)


def pick_rows(in_ref, out_ref, in_f, out_f):
    in_f[...] = in_ref[...].astype(F32)
    table = jnp.concatenate([in_f[rows_of(k, PEERS, 8), :] for k in range(4)], axis=1).astype(BF16)
    lane = lax.broadcasted_iota(jnp.int32, (PEERS, LANES), 1)
    for b in range(2):
        which = in_f[rows_of(4 + b, PEERS, 8), :].astype(jnp.int32)
        for h in range(2):
            chosen = (lane == 2 * which + h).astype(F32).astype(BF16)[:, :PEERS]
            picked = jnp.dot(chosen, table, preferred_element_type=F32)
            for k in range(4):
                out_f[rows_of(b * 8 + h * 4 + k, PEERS, 16), :] = picked[:, k * LANES:(k + 1) * LANES]
    out_ref[...] = out_f[...].astype(BF16)


def project(
    place_ref, order_ref, picked_ref, attn_ref, tokens_ref, one_ref, two_ref, three_ref, maps_ref, grad_ref, part_ref
):
    me = place_ref[0]
    width = grad_ref.shape[1]
    own = tokens_ref[:, pl.ds(pl.multiple_of(me * width, width), width)]
    grad_ref[pl.ds(pl.multiple_of(me * 64, 64), 64), :] = own
    for k, piece in ((1, one_ref), (2, two_ref), (3, three_ref)):
        first = pl.multiple_of(lax.bitwise_xor(me, k) * 64, 64)
        grad_ref[pl.ds(first, 64), :] = piece[:64, :]
    for c in range(BANDS):
        rows = picked_ref[c * 64:(c + 1) * 64, :].astype(F32).reshape(QUARTERS, 2, 8, LANES)
        for b in range(2):
            maps_ref[b * 32:(b + 1) * 32, c * LANES:(c + 1) * LANES] = rows[:, b].reshape(32, LANES).astype(BF16)
    row = lax.broadcasted_iota(jnp.int32, (32, BLOCK), 0)
    over_last = (((1,), (1,)), ((), ()))
    for b in range(2):
        maps = maps_ref[b * 32:(b + 1) * 32, :]
        block = slice(b * BLOCK, (b + 1) * BLOCK)
        inner = lax.dot_general(maps, attn_ref[block, :], over_last, preferred_element_type=F32)
        outer = lax.dot_general(maps, grad_ref[block, :], over_last, preferred_element_type=F32)
        part_ref[:, block] = jnp.where((row & 2) == 0, inner, outer)


def make_terms(own_ref, one_ref, two_ref, three_ref, live_ref, attn_ref, grad_ref, ranks_ref, term_ref):
    total = (own_ref[...] + one_ref[...]) + (two_ref[...] + three_ref[...])
    row = lax.broadcasted_iota(jnp.int32, (32, LANES), 0)
    terms = []
    for b in range(2):
        block = slice(b * BLOCK, (b + 1) * BLOCK)
        ranks = jnp.where(live_ref[b:b + 1, :] > 0, total[:, block], 0.0).astype(BF16)
        ranks_ref[:, block] = ranks
        down = jnp.dot(ranks, attn_ref[block, :], preferred_element_type=F32)
        up = jnp.dot(ranks, grad_ref[block, :], preferred_element_type=F32)
        terms.append((down, up))
    for c in range(BANDS):
        band = slice(c * LANES, (c + 1) * LANES)
        both = [
            adapter_scale * jnp.where((row & 2) == 0, up[:, band], down[:, band])
            for down, up in terms
        ]
        for q in range(QUARTERS):
            pair = jnp.concatenate([one[q * 8:(q + 1) * 8] for one in both], axis=0)
            term_ref[c * 64 + q * 16:c * 64 + (q + 1) * 16, :] = pair.astype(BF16)


def go_back(ranks_ref, maps_ref, back_ref):
    row = lax.broadcasted_iota(jnp.int32, (32, BLOCK), 0)
    over_first = (((0,), (0,)), ((), ()))
    for b in range(2):
        block = slice(b * BLOCK, (b + 1) * BLOCK)
        shifted = pltpu.roll(ranks_ref[:, block].astype(F32), 30, 0)
        outer = jnp.where((row & 2) == 0, shifted, 0.0).astype(BF16)
        back = lax.dot_general(outer, maps_ref[b * 32:(b + 1) * 32, :], over_first, preferred_element_type=F32)
        back_ref[block, :] = (adapter_scale * back).astype(BF16)


def add_up(in_ref, ids_ref, out_ref, in_f, ids_f):
    in_f[...] = in_ref[...].astype(F32)
    ids_f[...] = ids_ref[...].astype(F32)
    lane = lax.broadcasted_iota(jnp.int32, (PEERS, LANES), 1)
    over_first = (((0,), (0,)), ((), ()))
    total = jnp.zeros((LANES, 8 * LANES), F32)
    for b in range(2):
        which = ids_f[rows_of(4 + b, PEERS, 8), :].astype(jnp.int32)
        chosen = (lane == which).astype(F32).astype(BF16)
        terms = jnp.concatenate(
            [in_f[rows_of(b * 8 + k, PEERS, 16), :] for k in range(8)], axis=1
        ).astype(BF16)
        total += lax.dot_general(chosen, terms, over_first, preferred_element_type=F32)
    for k in range(8):
        out_ref[rows_of(k, 32, 8), :] = total[:32, k * LANES:(k + 1) * LANES]


def unpack(in_ref, down_ref, up_ref, rows_f):
    for m, map_ref in ((0, up_ref), (1, down_ref)):
        for i in range(2):
            rows_f[rows_of(i, PEERS, 2), :] = in_ref[rows_of(2 * m + i, PEERS, 4), :]
        for c in range(BANDS):
            map_ref[:, c * LANES:(c + 1) * LANES] = rows_f[c * 8:(c + 1) * 8, :]


def call(kernel, outs, specs, scratch=(), cost=None, limit=40 * MIB):
    return pl.pallas_call(
        kernel,
        out_shape=[jax.ShapeDtypeStruct(shape, dtype) for shape, dtype in outs],
        in_specs=specs,
        out_specs=[VMEM] * len(outs),
        scratch_shapes=scratch,
        compiler_params=pltpu.CompilerParams(vmem_limit_bytes=limit),
        cost_estimate=cost,
    )


def swap(x):
    chunks = x.reshape(PEERS, x.shape[0] // PEERS, LANES)
    return lax.all_to_all(chunks, "dp", 0, 0, tiled=True).reshape(x.shape)


def from_peer(x, k):
    return lax.ppermute(x, "tensor", [(i, i ^ k) for i in range(4)])


def per_device(attn, output_gradient, down_weight, up_weight, adapter_of_row, lengths):
    width = attn.shape[1]
    me = lax.axis_index("tensor")
    me = me.astype(jnp.int32).reshape(1)
    (packed,) = call(
        pack_tables,
        [((8 * PEERS, LANES), BF16)],
        [ANY] * 3,
        [
            pltpu.VMEM((8, width), BF16),
            pltpu.VMEM((8, width), BF16),
            pltpu.VMEM((2, BLOCK), jnp.int32),
            pltpu.VMEM((2 * PEERS, LANES), F32),
            pltpu.VMEM((8 * PEERS, LANES), F32),
            pltpu.SemaphoreType.DMA((3,)),
        ],
        limit=56 * MIB,
    )(down_weight, up_weight, adapter_of_row.reshape(2, BLOCK))
    near, far = call(
        cut_tokens,
        [((64, width), BF16), ((128, width), BF16)],
        [SMEM, ANY, ANY],
        [pltpu.SemaphoreType.DMA((3,))],
        limit=56 * MIB,
    )(me, output_gradient, packed)
    order = pl.pallas_call(
        copy_place,
        out_shape=jax.ShapeDtypeStruct((8, LANES), jnp.int32),
        in_specs=[SMEM],
        out_specs=VMEM,
        cost_estimate=pl.CostEstimate(flops=10 ** 10, bytes_accessed=8, transcendentals=0),
    )(me)
    live = (adapter_of_row >= 0) & (jnp.arange(2 * BLOCK, dtype=jnp.int32) < lengths[0])
    live = live.astype(F32).reshape(2, BLOCK)
    tables = swap(packed)
    tables, order = lax.optimization_barrier((tables, order))
    near, far = from_peer(near, 1), from_peer(far, 2)
    odd, live = lax.optimization_barrier((from_peer(far[64:], 1), live))
    pieces = [near, far, odd]
    (picked,) = call(
        pick_rows,
        [((16 * PEERS, LANES), BF16)],
        [VMEM],
        [pltpu.VMEM((8 * PEERS, LANES), F32), pltpu.VMEM((16 * PEERS, LANES), F32)],
    )(tables)
    picked = swap(picked)
    maps, grad, part = call(
        project,
        [((64, width), BF16), ((2 * BLOCK, width), BF16), ((32, 2 * BLOCK), F32)],
        [SMEM] + [VMEM] * 7,
    )(me, order, picked, attn, output_gradient, *pieces)
    parts = [part] + [from_peer(part, k) for k in (1, 2, 3)]
    ranks, terms = call(
        make_terms,
        [((32, 2 * BLOCK), BF16), ((16 * PEERS, LANES), BF16)],
        [VMEM] * 7,
    )(*parts, live, attn, grad)
    terms = swap(terms)
    (attention_gradient,) = call(
        go_back,
        [((2 * BLOCK, width), BF16)],
        [VMEM] * 2,
        cost=pl.CostEstimate(flops=2 * 32 * 256 * 2048, bytes_accessed=2 << 20, transcendentals=0),
    )(ranks, maps)
    (sums,) = call(
        add_up,
        [((4 * PEERS, LANES), F32)],
        [VMEM, VMEM],
        [pltpu.VMEM((16 * PEERS, LANES), F32), pltpu.VMEM((8 * PEERS, LANES), F32)],
    )(terms, tables)
    sums = swap(sums)
    grad_a, grad_b = call(
        unpack,
        [((8, width), F32), ((8, width), F32)],
        [VMEM],
        [pltpu.VMEM((2 * PEERS, LANES), F32)],
    )(sums)
    return attention_gradient, grad_a, grad_b


def solution(mesh):
    return jax.shard_map(
        per_device,
        mesh=mesh,
        in_specs=(
            P("dp", "tensor"),
            P(("dp", "tensor"), None),
            P("dp", "tensor"),
            P("dp", "tensor"),
            P("dp"),
            P("dp"),
        ),
        out_specs=(P("dp", "tensor"), P("dp", "tensor"), P("dp", "tensor")),
        check_vma=False,
    )
```

```python
import jax
import jax.numpy as jnp
from jax import lax
from jax.experimental import pallas as pl
from jax.experimental.pallas import tpu as pltpu
from jax.sharding import PartitionSpec as P

LANES = 128
BLOCK = 128
PEERS = 64
BANDS = 16
QUARTERS = 4

F32 = jnp.float32
BF16 = jnp.bfloat16

adapter_scale = 2.0

VMEM = pl.BlockSpec(memory_space=pltpu.VMEM)
ANY = pl.BlockSpec(memory_space=pl.ANY)
SMEM = pl.BlockSpec(memory_space=pltpu.SMEM)
MIB = 1024 * 1024


def rows_of(first, size, stride):
    return pl.ds(first, size, stride=stride)


def pack_tables(down_hbm, up_hbm, label_hbm, out_ref, down_ref, up_ref, label_ref, rows_f, out_f, sems):
    moves = ((label_hbm, label_ref), (down_hbm, down_ref), (up_hbm, up_ref))
    copies = [pltpu.make_async_copy(src, dst, sems.at[n]) for n, (src, dst) in enumerate(moves)]
    for copy in copies:
        copy.start()
    for b in range(2):
        out_f[rows_of(6 + b, PEERS, 8), :] = jnp.zeros((PEERS, LANES), F32)
    copies[0].wait()
    labels = label_ref[...]
    for b in range(2):
        which = jnp.maximum(labels[b:b + 1, 0:1], 0).astype(F32)
        out_f[rows_of(4 + b, PEERS, 8), :] = jnp.broadcast_to(which, (PEERS, LANES))
    for m, map_ref in enumerate((down_ref, up_ref)):
        copies[1 + m].wait()
        for c in range(BANDS):
            rows_f[c * 8:(c + 1) * 8, :] = map_ref[:, c * LANES:(c + 1) * LANES].astype(F32)
        for i in range(2):
            out_f[rows_of(2 * m + i, PEERS, 8), :] = rows_f[rows_of(i, PEERS, 2), :]
    out_ref[...] = out_f[...].astype(BF16)


def cut_tokens(place_ref, grad_hbm, packed_hbm, near_ref, far_ref, sems):
    width = near_ref.shape[1]
    copies = []
    for k, piece in ((2, far_ref.at[pl.ds(0, 64), :]), (3, far_ref.at[pl.ds(64, 64), :]), (1, near_ref)):
        first = pl.multiple_of(lax.bitwise_xor(place_ref[0], k) * width, width)
        copies.append(pltpu.make_async_copy(grad_hbm.at[:, pl.ds(first, width)], piece, sems.at[k - 1]))
    for copy in copies:
        copy.start()
    for copy in copies:
        copy.wait()


def copy_place(place_ref, out_ref):
    out_ref[...] = jnp.full(out_ref.shape, place_ref[0], jnp.int32)


def pick_rows(in_ref, out_hbm, in_f, out_f, out_ref, sems):
    in_f[...] = in_ref[...].astype(F32)
    table = jnp.concatenate([in_f[rows_of(k, PEERS, 8), :] for k in range(4)], axis=1).astype(BF16)
    lane = lax.broadcasted_iota(jnp.int32, (PEERS, LANES), 1)
    for b in range(2):
        which = in_f[rows_of(4 + b, PEERS, 8), :].astype(jnp.int32)
        for h in range(2):
            chosen = (lane == 2 * which + h).astype(F32).astype(BF16)[:, :PEERS]
            picked = jnp.dot(chosen, table, preferred_element_type=F32)
            for k in range(4):
                out_f[rows_of(b * 8 + h * 4 + k, PEERS, 16), :] = picked[:, k * LANES:(k + 1) * LANES]
    copies = []
    for n in range(4):
        part = slice(n * 256, (n + 1) * 256)
        out_ref[part, :] = out_f[part, :].astype(BF16)
        copies.append(pltpu.make_async_copy(out_ref.at[pl.ds(n * 256, 256), :], out_hbm.at[pl.ds(n * 256, 256), :], sems.at[n]))
        copies[-1].start()
    for copy in copies:
        copy.wait()


def project(
    place_ref, order_ref, picked_ref, attn_ref, tokens_ref, one_ref, two_ref, three_ref, maps_ref, grad_ref, part_ref
):
    me = place_ref[0]
    width = grad_ref.shape[1]
    own = tokens_ref[:, pl.ds(pl.multiple_of(me * width, width), width)]
    grad_ref[pl.ds(pl.multiple_of(me * 64, 64), 64), :] = own
    for k, piece in ((1, one_ref), (2, two_ref), (3, three_ref)):
        first = pl.multiple_of(lax.bitwise_xor(me, k) * 64, 64)
        grad_ref[pl.ds(first, 64), :] = piece[:64, :]
    for c in range(BANDS):
        rows = picked_ref[c * 64:(c + 1) * 64, :].astype(F32).reshape(QUARTERS, 2, 8, LANES)
        for b in range(2):
            maps_ref[b * 32:(b + 1) * 32, c * LANES:(c + 1) * LANES] = rows[:, b].reshape(32, LANES).astype(BF16)
    row = lax.broadcasted_iota(jnp.int32, (32, BLOCK), 0)
    over_last = (((1,), (1,)), ((), ()))
    for b in range(2):
        maps = maps_ref[b * 32:(b + 1) * 32, :]
        block = slice(b * BLOCK, (b + 1) * BLOCK)
        inner = lax.dot_general(maps, attn_ref[block, :], over_last, preferred_element_type=F32)
        outer = lax.dot_general(maps, grad_ref[block, :], over_last, preferred_element_type=F32)
        part_ref[:, block] = jnp.where((row & 2) == 0, inner, outer)


def make_terms(own_ref, one_ref, two_ref, three_ref, live_ref, attn_ref, grad_ref, ranks_ref, term_ref):
    total = (own_ref[...] + one_ref[...]) + (two_ref[...] + three_ref[...])
    row = lax.broadcasted_iota(jnp.int32, (32, LANES), 0)
    terms = []
    for b in range(2):
        block = slice(b * BLOCK, (b + 1) * BLOCK)
        ranks = jnp.where(live_ref[b:b + 1, :] > 0, total[:, block], 0.0).astype(BF16)
        ranks_ref[:, block] = ranks
        down = jnp.dot(ranks, attn_ref[block, :], preferred_element_type=F32)
        up = jnp.dot(ranks, grad_ref[block, :], preferred_element_type=F32)
        terms.append((down, up))
    for c in range(BANDS):
        band = slice(c * LANES, (c + 1) * LANES)
        both = [
            adapter_scale * jnp.where((row & 2) == 0, up[:, band], down[:, band])
            for down, up in terms
        ]
        for q in range(QUARTERS):
            pair = jnp.concatenate([one[q * 8:(q + 1) * 8] for one in both], axis=0)
            term_ref[c * 64 + q * 16:c * 64 + (q + 1) * 16, :] = pair.astype(BF16)


def go_back(ranks_ref, maps_ref, back_ref):
    row = lax.broadcasted_iota(jnp.int32, (32, BLOCK), 0)
    over_first = (((0,), (0,)), ((), ()))
    for b in range(2):
        block = slice(b * BLOCK, (b + 1) * BLOCK)
        shifted = pltpu.roll(ranks_ref[:, block].astype(F32), 30, 0)
        outer = jnp.where((row & 2) == 0, shifted, 0.0).astype(BF16)
        back = lax.dot_general(outer, maps_ref[b * 32:(b + 1) * 32, :], over_first, preferred_element_type=F32)
        back_ref[block, :] = (adapter_scale * back).astype(BF16)


def add_up(in_ref, ids_ref, out_ref, in_f, ids_f):
    in_f[...] = in_ref[...].astype(F32)
    ids_f[...] = ids_ref[...].astype(F32)
    lane = lax.broadcasted_iota(jnp.int32, (PEERS, LANES), 1)
    over_first = (((0,), (0,)), ((), ()))
    total = jnp.zeros((LANES, 8 * LANES), F32)
    for b in range(2):
        which = ids_f[rows_of(4 + b, PEERS, 8), :].astype(jnp.int32)
        chosen = (lane == which).astype(F32).astype(BF16)
        terms = jnp.concatenate(
            [in_f[rows_of(b * 8 + k, PEERS, 16), :] for k in range(8)], axis=1
        ).astype(BF16)
        total += lax.dot_general(chosen, terms, over_first, preferred_element_type=F32)
    for k in range(8):
        out_ref[rows_of(k, 32, 8), :] = total[:32, k * LANES:(k + 1) * LANES]


def unpack(in_ref, down_ref, up_ref, rows_f):
    for m, map_ref in ((0, up_ref), (1, down_ref)):
        for i in range(2):
            rows_f[rows_of(i, PEERS, 2), :] = in_ref[rows_of(2 * m + i, PEERS, 4), :]
        for c in range(BANDS):
            map_ref[:, c * LANES:(c + 1) * LANES] = rows_f[c * 8:(c + 1) * 8, :]


def call(kernel, outs, specs, scratch=(), cost=None, limit=40 * MIB, places=None):
    return pl.pallas_call(
        kernel,
        out_shape=[jax.ShapeDtypeStruct(shape, dtype) for shape, dtype in outs],
        in_specs=specs,
        out_specs=places or [VMEM] * len(outs),
        scratch_shapes=scratch,
        compiler_params=pltpu.CompilerParams(vmem_limit_bytes=limit),
        cost_estimate=cost,
    )


def swap(x):
    chunks = x.reshape(PEERS, x.shape[0] // PEERS, LANES)
    return lax.all_to_all(chunks, "dp", 0, 0, tiled=True).reshape(x.shape)


def from_peer(x, k):
    return lax.ppermute(x, "tensor", [(i, i ^ k) for i in range(4)])


def per_device(attn, output_gradient, down_weight, up_weight, adapter_of_row, lengths):
    width = attn.shape[1]
    me = lax.axis_index("tensor")
    me = me.astype(jnp.int32).reshape(1)
    (packed,) = call(
        pack_tables,
        [((8 * PEERS, LANES), BF16)],
        [ANY] * 3,
        [
            pltpu.VMEM((8, width), BF16),
            pltpu.VMEM((8, width), BF16),
            pltpu.VMEM((2, BLOCK), jnp.int32),
            pltpu.VMEM((2 * PEERS, LANES), F32),
            pltpu.VMEM((8 * PEERS, LANES), F32),
            pltpu.SemaphoreType.DMA((3,)),
        ],
        limit=56 * MIB,
    )(down_weight, up_weight, adapter_of_row.reshape(2, BLOCK))
    near, far = call(
        cut_tokens,
        [((64, width), BF16), ((128, width), BF16)],
        [SMEM, ANY, ANY],
        [pltpu.SemaphoreType.DMA((3,))],
        limit=56 * MIB,
    )(me, output_gradient, packed)
    order = pl.pallas_call(
        copy_place,
        out_shape=jax.ShapeDtypeStruct((8, LANES), jnp.int32),
        in_specs=[SMEM],
        out_specs=VMEM,
        cost_estimate=pl.CostEstimate(flops=10 ** 10, bytes_accessed=8, transcendentals=0),
    )(me)
    live = (adapter_of_row >= 0) & (jnp.arange(2 * BLOCK, dtype=jnp.int32) < lengths[0])
    live = live.astype(F32).reshape(2, BLOCK)
    tables = swap(packed)
    tables, order = lax.optimization_barrier((tables, order))
    near, far = from_peer(near, 1), from_peer(far, 2)
    odd, live = lax.optimization_barrier((from_peer(far[64:], 1), live))
    pieces = [near, far, odd]
    (picked,) = call(
        pick_rows,
        [((16 * PEERS, LANES), BF16)],
        [VMEM],
        [
            pltpu.VMEM((8 * PEERS, LANES), F32),
            pltpu.VMEM((16 * PEERS, LANES), F32),
            pltpu.VMEM((16 * PEERS, LANES), BF16),
            pltpu.SemaphoreType.DMA((4,)),
        ],
        places=[ANY],
    )(tables)
    picked = swap(picked)
    maps, grad, part = call(
        project,
        [((64, width), BF16), ((2 * BLOCK, width), BF16), ((32, 2 * BLOCK), F32)],
        [SMEM] + [VMEM] * 7,
    )(me, order, picked, attn, output_gradient, *pieces)
    parts = [part] + [from_peer(part, k) for k in (1, 2, 3)]
    ranks, terms = call(
        make_terms,
        [((32, 2 * BLOCK), BF16), ((16 * PEERS, LANES), BF16)],
        [VMEM] * 7,
    )(*parts, live, attn, grad)
    terms = swap(terms)
    (attention_gradient,) = call(
        go_back,
        [((2 * BLOCK, width), BF16)],
        [VMEM] * 2,
        cost=pl.CostEstimate(flops=2 * 32 * 256 * 2048, bytes_accessed=2 << 20, transcendentals=0),
    )(ranks, maps)
    (sums,) = call(
        add_up,
        [((4 * PEERS, LANES), F32)],
        [VMEM, VMEM],
        [pltpu.VMEM((16 * PEERS, LANES), F32), pltpu.VMEM((8 * PEERS, LANES), F32)],
    )(terms, tables)
    sums = swap(sums)
    grad_a, grad_b = call(
        unpack,
        [((8, width), F32), ((8, width), F32)],
        [VMEM],
        [pltpu.VMEM((2 * PEERS, LANES), F32)],
    )(sums)
    return attention_gradient, grad_a, grad_b


def solution(mesh):
    return jax.shard_map(
        per_device,
        mesh=mesh,
        in_specs=(
            P("dp", "tensor"),
            P(("dp", "tensor"), None),
            P("dp", "tensor"),
            P("dp", "tensor"),
            P("dp"),
            P("dp"),
        ),
        out_specs=(P("dp", "tensor"), P("dp", "tensor"), P("dp", "tensor")),
        check_vma=False,
    )
```
